128 devices in a mesh: band: 2 (over z_lo), prow: 4 (over x), pcol: 16 (over y, z_hi, core).
Axes of the slice: x: 4, y: 4, z: 4 (z_hi: 2, z_lo: 2; z = z_hi * 2 + z_lo), core: 2. Of those that a mesh axis runs over, the one named last changes fastest.
Arguments:
- orbitals: float32 [4, 192, 192, 192], P('band', 'prow', 'pcol'), may hold values from -6 to 6
- kernel: float32 [192, 192, 192], P('prow', 'pcol'), as said below
- plan: int32 [4], replicated, may hold values from 0 to 3, each once
- occupation: int32 [4], replicated, may hold values 0 or 1
Outputs:
- exchange_orbitals: float32 [4, 192, 192, 192], P('band', 'prow', 'pcol')
The draws below stay inside these ranges and needn't reach their ends.
Inputs may be any that keep to these rules, and one draw needn't show every extreme that they name: `plan`: a permutation of the blocks; entry e names block e % (2) of band group e // 2; this window treats the blocks of its first 2 entries. kernel at (ky, kz, kx) equals kernel at (-ky, -kz, -kx), indices taken modulo 192.
All inputs are finite; a program needn't handle non-finite values.
Results may differ from the reference program's by a relative error of at most 0.00014.
Values sent between devices are 32-bit elements; how exact they have to be, the bound alone decides.
A program may use at most 128 MiB of HBM per device.

```python
import jax
import jax.numpy as jnp
from jax import lax

GRID = 192
BANDS_DEV = 2
IBLK = 1
ROUNDS = 2
NBANDS = 4
NBLOCKS = 4


def draw_kernel(key, part):
    raw = jax.random.uniform(key, (GRID, GRID, GRID), jnp.float32, 0.1, 1.9)
    mirrored = jnp.roll(jnp.flip(raw, (0, 1, 2)), 1, (0, 1, 2))
    return 0.5 * (raw + mirrored)


def place_ends(entries, key, least, high):
    longest = entries.shape.index(max(entries.shape))
    spots = []
    for shift in (0, 1):
        where = [jax.random.randint(jax.random.fold_in(key, axis), (), 0, length) for axis, length in enumerate(entries.shape)]
        where[longest] = (where[longest] + shift) % entries.shape[longest]
        spots.append(tuple(where))
    return entries.at[spots[0]].set(least).at[spots[1]].set(high)


def shard_levels(rng, shape, split, low, largest):
    def one(dim, shards_of):
        draws = jax.random.uniform(jax.random.fold_in(jax.random.fold_in(rng, 6), dim), (shards_of,), jnp.float32, low / len(split), largest / len(split))
        return jnp.repeat(jnp.exp(draws), shape[dim] // shards_of).reshape((-1,) + (1,) * (len(shape) - dim - 1))

    level = one(*split[0])
    for cut in split[1:]:
        level = level * one(*cut)
    return level


def scatter_about(key, dims, width, reach, pieces=(), kind=jnp.bfloat16):
    factor_of = shard_levels(key, dims, pieces, -0.22, 0.18) if pieces else 1.0
    entries = jax.random.normal(key, dims, jnp.float32) * width * factor_of
    return jnp.minimum(jnp.maximum(entries, -reach), reach).astype(kind)


def setup_inputs(seed: int = 0) -> dict:
    key_list = jax.random.split(jax.random.key(seed), 5)
    return {
        "orbitals": scatter_about(key_list[0], (NBANDS, GRID, GRID, GRID), 1.0, 6.0, ((0, 2), (1, 4), (2, 16)), jnp.float32),
        "kernel": draw_kernel(jax.random.fold_in(key_list[4], 71), 0),
        "plan": jax.random.permutation(key_list[2], NBLOCKS).astype(jnp.int32),
        "occupation": place_ends((jax.random.randint(key_list[3], (NBANDS,), 0, 4) < 3).astype(jnp.int32), jax.random.fold_in(key_list[3], 1), 0, 1),
    }


def reference(orbitals, kernel, plan, occupation):
    kernel_xyz = jnp.transpose(kernel, (2, 0, 1))
    per_owner = BANDS_DEV // IBLK
    summed = jnp.zeros(orbitals.shape, jnp.float32)
    for round_id in range(ROUNDS):
        block_id = plan[round_id]
        first_band = ((block_id // per_owner) * BANDS_DEV + (block_id % per_owner) * IBLK).astype(jnp.int32)
        block = lax.dynamic_slice_in_dim(orbitals, first_band, IBLK, 0)
        weights = lax.dynamic_slice_in_dim(occupation, first_band, IBLK, 0).astype(jnp.float32) * -0.25
        for member in range(IBLK):
            source = block[member]

            def pair_term(target, source=source):
                density = source * target
                field = jnp.real(jnp.fft.ifftn(kernel_xyz * jnp.fft.fftn(density)))
                return field * source

            summed = summed + weights[member] * lax.map(pair_term, orbitals)
    return summed
```

```python
import functools

import jax
import jax.numpy as jnp
import ml_dtypes
import numpy as np
from jax import lax
from jax.experimental import pallas as pl
from jax.experimental.pallas import tpu as pltpu
from jax.sharding import PartitionSpec as P

N = 192
PC = 16
PR = 4
YB = 12
XB = 48
PARTS = 3
K4 = 4
W = 384
CH = 24
F32 = jnp.float32
BF16 = jnp.bfloat16
MESH = pl.DeviceIdType.MESH


def split_table(table):
    high = table.astype(np.float32).astype(ml_dtypes.bfloat16)
    low = (table - high.astype(np.float64)).astype(np.float32).astype(ml_dtypes.bfloat16)
    return high, low


def complex_table(out_part, out_freq, in_part, in_point, sign):
    angle = 2.0 * np.pi * ((out_freq[:, None] * in_point[None, :]) % N) / N
    cosine, sine = np.cos(angle), sign * np.sin(angle)
    op, ip = out_part[:, None], in_part[None, :]
    return np.where(op == ip, cosine, np.where(op == 0, -sine, sine))


def grid(*sizes):
    return [a.reshape(-1) for a in np.meshgrid(*[np.arange(s) for s in sizes], indexing="ij")]


def make_tables():
    z_part = np.concatenate([np.zeros(128), np.ones(128), np.zeros(64), np.ones(64)]).astype(int)
    z_point = np.concatenate([np.arange(128)] * 2 + [np.arange(128, 192)] * 2)
    c, k4, s, q = grid(2, K4, PARTS, PC)
    kz = q * YB + s * K4 + k4
    t1 = complex_table(c, kz, z_part, z_point, -1)
    k4, c, s, q = grid(K4, 2, PARTS, PC)
    kz = q * YB + s * K4 + k4
    t5 = -0.25 * complex_table(z_part, z_point, c, kz, 1).T
    p, y, yc = grid(PC, YB, 2)
    y_point = p * YB + y
    u, uc, k = grid(PR, 2, XB)
    ky = u * XB + k
    t2 = complex_table(uc, ky, yc, y_point, -1).T
    t4 = complex_table(yc, y_point, uc, ky, 1)
    xc, kx = grid(2, N)
    t3 = complex_table(xc, kx, uc, ky, -1)
    t3i = complex_table(uc, ky, xc, kx, 1) / float(N) ** 3
    return [part for t in (t1, t2, t3, t3i, t4, t5) for part in split_table(t)]


def halves(x):
    high = x.astype(BF16)
    return high, (x - high.astype(F32)).astype(BF16)


def dot3(left, right, dims):
    def dot(a, b):
        return lax.dot_general(a, b, (dims, ((), ())), preferred_element_type=F32)

    return dot(left[0], right[0]) + (dot(left[0], right[1]) + dot(left[1], right[0]))


NN = ((1,), (0,))
NT = ((1,), (1,))


def swap_slots(blocks):
    slot = lax.broadcasted_iota(jnp.int32, (XB, W), 1) // XB
    blocks = list(blocks)
    for bit in (1, 2, 4):
        keep = (slot & bit) == 0
        for m in range(8):
            if m & bit == 0:
                a, b = blocks[m], blocks[m + bit]
                blocks[m] = jnp.where(keep, a, pltpu.roll(b, XB * bit, 1))
                blocks[m + bit] = jnp.where(keep, pltpu.roll(a, W - XB * bit, 1), b)
    return blocks


def body(
    c_ref, phi_ref, ker_ref, t1h, t1l, t2h, t2l, t3h, t3l, t3ih, t3il, t4h, t4l, t5h, t5l,
    out_ref,
    psi, s1, r1, s2, r2, s3, r3, s4, r4,
    psi_send, psi_recv, own_sem, send_sem, recv_sem,
):
    me_p = lax.axis_index("pcol")
    me_r = lax.axis_index("prow")
    partner = 1 - lax.axis_index("band")

    barrier = pltpu.get_barrier_semaphore()

    def greet_p(k, _):
        pl.semaphore_signal(barrier, inc=1, device_id={"pcol": lax.rem(me_p + k, PC)}, device_id_type=MESH)
        return 0

    def greet_r(k, _):
        pl.semaphore_signal(barrier, inc=1, device_id={"prow": lax.rem(me_r + k, PR)}, device_id_type=MESH)
        return 0

    lax.fori_loop(1, PC, greet_p, 0)
    lax.fori_loop(1, PR, greet_r, 0)
    pl.semaphore_signal(barrier, inc=1, device_id={"band": partner}, device_id_type=MESH)
    pl.semaphore_wait(barrier, PC - 1 + PR - 1 + 1)

    groups = 3
    rows = YB // groups * XB

    def psi_copy(g):
        return pltpu.make_async_remote_copy(
            src_ref=c_ref.at[pl.ds(g * rows, rows)],
            dst_ref=psi.at[pl.ds(g * rows, rows)],
            send_sem=psi_send.at[g],
            recv_sem=psi_recv.at[g],
            device_id={"band": partner},
            device_id_type=MESH,
        )

    for g in range(groups):
        psi_copy(g).start()

    def pcol_start(e, s, src, dst):
        mine = pl.ds(me_p * CH, CH)

        def send(k, _):
            to = lax.rem(me_p + k, PC)
            pltpu.make_async_remote_copy(
                src_ref=src.at[s, :, pl.ds(to * CH, CH), :],
                dst_ref=dst.at[s, :, mine, :],
                send_sem=send_sem.at[e, s],
                recv_sem=recv_sem.at[e, s],
                device_id={"pcol": to},
                device_id_type=MESH,
            ).start()
            return 0

        lax.fori_loop(1, PC, send, 0)
        pltpu.make_async_copy(src.at[s, :, mine, :], dst.at[s, :, mine, :], own_sem.at[e, s]).start()

    def pcol_wait(e, s, src, dst):
        mine = pl.ds(me_p * CH, CH)
        pltpu.make_async_copy(src.at[s, :, mine, :], dst.at[s, :, mine, :], own_sem.at[e, s]).wait()
        others = dst.at[s, :, pl.ds(0, (PC - 1) * CH), :]
        pltpu.make_async_copy(others, others, recv_sem.at[e, s]).wait()

    def pcol_sent(e, s, src):
        others = src.at[s, :, pl.ds(0, (PC - 1) * CH), :]
        pltpu.make_async_copy(others, others, send_sem.at[e, s]).wait()

    def prow_start(e, s, src, dst):
        def send(k, _):
            to = lax.rem(me_r + k, PR)
            pltpu.make_async_remote_copy(
                src_ref=src.at[s, to],
                dst_ref=dst.at[s, me_r],
                send_sem=send_sem.at[e, s],
                recv_sem=recv_sem.at[e, s],
                device_id={"prow": to},
                device_id_type=MESH,
            ).start()
            return 0

        lax.fori_loop(1, PR, send, 0)
        pltpu.make_async_copy(src.at[s, me_r], dst.at[s, me_r], own_sem.at[e, s]).start()

    def prow_wait(e, s, src, dst):
        pltpu.make_async_copy(src.at[s, me_r], dst.at[s, me_r], own_sem.at[e, s]).wait()
        others = dst.at[s, pl.ds(0, PR - 1)]
        pltpu.make_async_copy(others, others, recv_sem.at[e, s]).wait()

    def prow_sent(e, s, src):
        others = src.at[s, pl.ds(0, PR - 1)]
        pltpu.make_async_copy(others, others, send_sem.at[e, s]).wait()

    def forward_z(y, _):
        at = pl.ds(pl.multiple_of(y * XB, 16), XB)
        source = c_ref[at, :] + psi[at, :]
        psi[at, :] = source
        dens = jnp.concatenate(
            [phi_ref[pl.ds(pl.multiple_of(y * 2 * XB + j * XB, 16), XB), :] * source for j in range(2)], axis=0
        )
        spec = dot3((t1h[...], t1l[...]), halves(dens), NT)
        for c in range(2):
            base = c * K4 * XB
            wide = jnp.concatenate([spec[base + k * XB : base + (k + 1) * XB] for k in range(K4)], axis=1)
            for s in range(PARTS):
                for lane in range(3):
                    s1[s, lane, pl.ds(y * 2 + c, PC, stride=CH), :] = wide[
                        s * PC : (s + 1) * PC, lane * 128 : (lane + 1) * 128
                    ]
        return 0

    for g in range(groups):
        psi_copy(g).wait_recv()
        lax.fori_loop(g * (YB // groups), (g + 1) * (YB // groups), forward_z, 0)
    for s in range(PARTS):
        pcol_start(0, s, s1, r1)

    def forward_y(s):
        pcol_wait(0, s, s1, r1)
        turned = jnp.concatenate([r1[s, lane].T for lane in range(3)], axis=0)
        spec = dot3(halves(turned), (t2h[...], t2l[...]), NN)
        spec = swap_slots([spec[m * XB : (m + 1) * XB] for m in range(8)])
        for w in range(8):
            s2[s, w // 2, (w % 2) * XB : (w % 2 + 1) * XB, :] = spec[w]
        prow_start(1, s, s2, r2)

    def middle_x(s):
        prow_wait(1, s, s2, r2)
        data = r2[s].reshape(W, W)
        freq = dot3((t3h[...], t3l[...]), halves(data), NN)
        weight = ker_ref[s]
        freq = jnp.concatenate([freq[:N] * weight, freq[N:] * weight], axis=0)
        back = dot3((t3ih[...], t3il[...]), halves(freq), NN)
        s3[s] = back.reshape(PR, 2 * XB, W)
        prow_start(2, s, s3, r3)

    def backward_y(s):
        prow_wait(2, s, s3, r3)
        data = swap_slots([r3[s, w // 2, (w % 2) * XB : (w % 2 + 1) * XB, :] for w in range(8)])
        data = jnp.concatenate(data, axis=0)
        back = dot3((t4h[...], t4l[...]), halves(data), NT)
        for lane in range(3):
            s4[s, lane] = back[:, lane * 128 : (lane + 1) * 128]
        pcol_start(3, s, s4, r4)

    forward_y(0)
    forward_y(1)
    middle_x(0)
    forward_y(2)
    middle_x(1)
    backward_y(0)
    middle_x(2)
    backward_y(1)
    backward_y(2)
    for s in range(PARTS):
        pcol_wait(3, s, s4, r4)

    def backward_z(y, _):
        near = jnp.concatenate(
            [
                jnp.concatenate([r4[s, lane, pl.ds(y * 2 + c, PC, stride=CH), :] for lane in range(3)], axis=1)
                for c in range(2)
                for s in range(PARTS)
            ],
            axis=0,
        )
        lhs = jnp.concatenate([near[:, k * 2 * XB : (k + 1) * 2 * XB] for k in range(K4)], axis=0)
        lhs = jnp.concatenate([lhs, jnp.zeros((W, 32), F32)], axis=1)
        field = dot3(halves(lhs.T[: 2 * XB]), (t5h[...], t5l[...]), NN)
        source = psi[pl.ds(pl.multiple_of(y * XB, 16), XB), :]
        for j in range(2):
            term = field[j * XB : (j + 1) * XB] * source
            rest = term[:, 256:]
            at = pl.ds(pl.multiple_of(y * 2 * XB + j * XB, 16), XB)
            out_ref[at, :128] = term[:, :128] + term[:, 128:256]
            out_ref[at, 128:] = (rest + pltpu.roll(rest, 64, 1))[:, :64]
        return 0

    lax.fori_loop(0, YB, backward_z, 0)
    for g in range(groups):
        psi_copy(g).wait_send()
    for s in range(PARTS):
        pcol_sent(0, s, s1)
        prow_sent(1, s, s2)
        prow_sent(2, s, s3)
        pcol_sent(3, s, s4)


def spread(a):
    return jnp.concatenate([a[..., :128], a[..., :128], a[..., 128:], a[..., 128:]], axis=-1)


def on_device(orbitals, kernel, plan, occupation):
    laid = jnp.transpose(orbitals, (2, 0, 1, 3))
    group = lax.axis_index("band")
    own = []
    for r in range(2):
        block = plan[r]
        occupied = lax.dynamic_index_in_dim(occupation, block, 0, keepdims=False) != 0
        mine = jnp.logical_and(block // 2 == group, occupied)
        band = lax.dynamic_index_in_dim(laid, block % 2, 1, keepdims=False)
        own.append(jnp.where(mine, band, jnp.zeros_like(band)))
    c = jnp.concatenate([own[0][..., :128], own[1][..., :128], own[0][..., 128:], own[1][..., 128:]], axis=-1)
    c = c.reshape(YB * XB, W)
    phi = spread(laid).reshape(YB * 2 * XB, W)
    ker = jnp.transpose(kernel.reshape(XB, PARTS, K4, N), (1, 3, 2, 0))
    ker = jnp.broadcast_to(ker[:, :, :, None, :], (PARTS, N, K4, 2, XB)).reshape(PARTS, N, W)
    tables = [jnp.asarray(t) for t in make_tables()]
    pcol_buf = pltpu.VMEM((PARTS, 3, PC * CH, 128), F32)
    prow_buf = pltpu.VMEM((PARTS, PR, 2 * XB, W), F32)
    vmem = pl.BlockSpec(memory_space=pltpu.VMEM)
    out = pl.pallas_call(
        body,
        out_shape=jax.ShapeDtypeStruct((YB * 2 * XB, N), F32),
        in_specs=[vmem] * 15,
        out_specs=vmem,
        scratch_shapes=[
            pltpu.VMEM((YB * XB, W), F32),
            pcol_buf, pcol_buf, prow_buf, prow_buf, prow_buf, prow_buf, pcol_buf, pcol_buf,
            pltpu.SemaphoreType.DMA((3,)),
            pltpu.SemaphoreType.DMA((3,)),
            pltpu.SemaphoreType.DMA((4, PARTS)),
            pltpu.SemaphoreType.DMA((4, PARTS)),
            pltpu.SemaphoreType.DMA((4, PARTS)),
        ],
        compiler_params=pltpu.CompilerParams(
            collective_id=0, has_side_effects=True, vmem_limit_bytes=56 * 2**20
        ),
    )(c, phi, ker, *tables)
    return jnp.transpose(out.reshape(YB, 2, XB, N), (1, 2, 0, 3))


def solution(mesh):
    return jax.shard_map(
        on_device,
        mesh=mesh,
        in_specs=(P("band", "prow", "pcol", None), P("prow", "pcol", None), P(), P()),
        out_specs=P("band", "prow", "pcol", None),
        check_vma=False,
    )
```

```python
import functools

import jax
import jax.numpy as jnp
import ml_dtypes
import numpy as np
from jax import lax
from jax.experimental import pallas as pl
from jax.experimental.pallas import tpu as pltpu
from jax.sharding import PartitionSpec as P

N = 192
PC = 16
PR = 4
YB = 12
XB = 48
PARTS = 3
K4 = 4
W = 384
CH = 24
F32 = jnp.float32
BF16 = jnp.bfloat16
MESH = pl.DeviceIdType.MESH


def split_table(table):
    high = table.astype(np.float32).astype(ml_dtypes.bfloat16)
    low = (table - high.astype(np.float64)).astype(np.float32).astype(ml_dtypes.bfloat16)
    return high, low


def complex_table(out_part, out_freq, in_part, in_point, sign):
    angle = 2.0 * np.pi * ((out_freq[:, None] * in_point[None, :]) % N) / N
    cosine, sine = np.cos(angle), sign * np.sin(angle)
    op, ip = out_part[:, None], in_part[None, :]
    return np.where(op == ip, cosine, np.where(op == 0, -sine, sine))


def grid(*sizes):
    return [a.reshape(-1) for a in np.meshgrid(*[np.arange(s) for s in sizes], indexing="ij")]


def make_tables():
    z_part = np.concatenate([np.zeros(128), np.ones(128), np.zeros(64), np.ones(64)]).astype(int)
    z_point = np.concatenate([np.arange(128)] * 2 + [np.arange(128, 192)] * 2)
    c, k4, s, q = grid(2, K4, PARTS, PC)
    kz = q * YB + s * K4 + k4
    t1 = complex_table(c, kz, z_part, z_point, -1)
    k4, c, s, q = grid(K4, 2, PARTS, PC)
    kz = q * YB + s * K4 + k4
    t5 = -0.25 * complex_table(z_part, z_point, c, kz, 1).T
    p, y, yc = grid(PC, YB, 2)
    y_point = p * YB + y
    u, uc, k = grid(PR, 2, XB)
    ky = u * XB + k
    t2 = complex_table(uc, ky, yc, y_point, -1).T
    t4 = complex_table(yc, y_point, uc, ky, 1)
    xc, kx = grid(2, N)
    t3 = complex_table(xc, kx, uc, ky, -1)
    t3i = complex_table(uc, ky, xc, kx, 1) / float(N) ** 3
    return [part for t in (t1, t2, t3, t3i, t4, t5) for part in split_table(t)]


def halves(x):
    high = x.astype(BF16)
    return high, (x - high.astype(F32)).astype(BF16)


def dot3(left, right, dims):
    def dot(a, b):
        return lax.dot_general(a, b, (dims, ((), ())), preferred_element_type=F32)

    return dot(left[0], right[0]) + (dot(left[0], right[1]) + dot(left[1], right[0]))


NN = ((1,), (0,))
NT = ((1,), (1,))


def swap_slots(blocks):
    slot = lax.broadcasted_iota(jnp.int32, (XB, W), 1) // XB
    blocks = list(blocks)
    for bit in (1, 2, 4):
        keep = (slot & bit) == 0
        for m in range(8):
            if m & bit == 0:
                a, b = blocks[m], blocks[m + bit]
                blocks[m] = jnp.where(keep, a, pltpu.roll(b, XB * bit, 1))
                blocks[m + bit] = jnp.where(keep, pltpu.roll(a, W - XB * bit, 1), b)
    return blocks


def body(
    plan_ref, occ_ref, orb_hbm, ker_hbm, tables_hbm,
    out_ref,
    orb, ker, weight, tables, mine, psi, s1, r1, s2, r2, s3, r3, s4, r4,
    load_sem, psi_send, psi_recv, own_sem, send_sem, recv_sem,
):
    def table(t):
        return tables[2 * t], tables[2 * t + 1]

    loads = [pltpu.make_async_copy(orb_hbm, orb, load_sem.at[0])]
    loads += [
        pltpu.make_async_copy(
            tables_hbm.at[pl.ds(2 * t, 2)], tables.at[pl.ds(2 * t, 2)], load_sem.at[2 + t]
        )
        for t in range(6)
    ]
    loads.append(pltpu.make_async_copy(ker_hbm, ker, load_sem.at[1]))
    for load in loads:
        load.start()

    me_p = lax.axis_index("pcol")
    me_r = lax.axis_index("prow")
    me_b = lax.axis_index("band")
    partner = 1 - me_b

    barrier = pltpu.get_barrier_semaphore()

    def greet_p(k, _):
        pl.semaphore_signal(barrier, inc=1, device_id={"pcol": lax.rem(me_p + k, PC)}, device_id_type=MESH)
        return 0

    def greet_r(k, _):
        pl.semaphore_signal(barrier, inc=1, device_id={"prow": lax.rem(me_r + k, PR)}, device_id_type=MESH)
        return 0

    lax.fori_loop(1, PC, greet_p, 0)
    lax.fori_loop(1, PR, greet_r, 0)
    pl.semaphore_signal(barrier, inc=1, device_id={"band": partner}, device_id_type=MESH)
    pl.semaphore_wait(barrier, PC - 1 + PR - 1 + 1)

    groups = 3
    rows = YB // groups * XB

    def psi_copy(g):
        return pltpu.make_async_remote_copy(
            src_ref=mine.at[pl.ds(g * rows, rows)],
            dst_ref=psi.at[pl.ds(g * rows, rows)],
            send_sem=psi_send.at[g],
            recv_sem=psi_recv.at[g],
            device_id={"band": partner},
            device_id_type=MESH,
        )

    share = [
        [
            jnp.where(
                jnp.logical_and(plan_ref[r] == 2 * me_b + b, occ_ref[2 * me_b + b] != 0),
                jnp.float32(1.0), jnp.float32(0.0),
            )
            for b in range(2)
        ]
        for r in range(2)
    ]

    def own_source(y, _):
        at = pl.ds(pl.multiple_of(y * XB, 16), XB)
        bands = [orb[b, at, :] for b in range(2)]
        parts = [share[r][0] * bands[0] + share[r][1] * bands[1] for r in range(2)]
        mine[at, :128] = parts[0][:, :128]
        mine[at, 128:256] = parts[1][:, :128]
        mine[at, 256:] = jnp.concatenate([parts[0][:, 128:], parts[1][:, 128:]], axis=1)
        return 0

    loads[0].wait()
    for g in range(groups):
        lax.fori_loop(g * (YB // groups), (g + 1) * (YB // groups), own_source, 0)
        psi_copy(g).start()
    loads[1].wait()

    def pcol_start(e, s, src, dst):
        mine = pl.ds(me_p * CH, CH)

        def send(k, _):
            to = lax.rem(me_p + k, PC)
            pltpu.make_async_remote_copy(
                src_ref=src.at[s, :, pl.ds(to * CH, CH), :],
                dst_ref=dst.at[s, :, mine, :],
                send_sem=send_sem.at[e, s],
                recv_sem=recv_sem.at[e, s],
                device_id={"pcol": to},
                device_id_type=MESH,
            ).start()
            return 0

        lax.fori_loop(1, PC, send, 0)
        pltpu.make_async_copy(src.at[s, :, mine, :], dst.at[s, :, mine, :], own_sem.at[e, s]).start()

    def pcol_wait(e, s, src, dst):
        mine = pl.ds(me_p * CH, CH)
        pltpu.make_async_copy(src.at[s, :, mine, :], dst.at[s, :, mine, :], own_sem.at[e, s]).wait()
        others = dst.at[s, :, pl.ds(0, (PC - 1) * CH), :]
        pltpu.make_async_copy(others, others, recv_sem.at[e, s]).wait()

    def pcol_sent(e, s, src):
        others = src.at[s, :, pl.ds(0, (PC - 1) * CH), :]
        pltpu.make_async_copy(others, others, send_sem.at[e, s]).wait()

    def prow_start(e, s, src, dst):
        def send(k, _):
            to = lax.rem(me_r + k, PR)
            pltpu.make_async_remote_copy(
                src_ref=src.at[s, to],
                dst_ref=dst.at[s, me_r],
                send_sem=send_sem.at[e, s],
                recv_sem=recv_sem.at[e, s],
                device_id={"prow": to},
                device_id_type=MESH,
            ).start()
            return 0

        lax.fori_loop(1, PR, send, 0)
        pltpu.make_async_copy(src.at[s, me_r], dst.at[s, me_r], own_sem.at[e, s]).start()

    def prow_wait(e, s, src, dst):
        pltpu.make_async_copy(src.at[s, me_r], dst.at[s, me_r], own_sem.at[e, s]).wait()
        others = dst.at[s, pl.ds(0, PR - 1)]
        pltpu.make_async_copy(others, others, recv_sem.at[e, s]).wait()

    def prow_sent(e, s, src):
        others = src.at[s, pl.ds(0, PR - 1)]
        pltpu.make_async_copy(others, others, send_sem.at[e, s]).wait()

    def forward_z(y, _):
        at = pl.ds(pl.multiple_of(y * XB, 16), XB)
        source = mine[at, :] + psi[at, :]
        psi[at, :] = source
        dens = jnp.concatenate([spread(orb[j, at, :]) * source for j in range(2)], axis=0)
        spec = dot3(table(0), halves(dens), NT)
        for c in range(2):
            base = c * K4 * XB
            wide = jnp.concatenate([spec[base + k * XB : base + (k + 1) * XB] for k in range(K4)], axis=1)
            for s in range(PARTS):
                for lane in range(3):
                    s1[s, lane, pl.ds(y * 2 + c, PC, stride=CH), :] = wide[
                        s * PC : (s + 1) * PC, lane * 128 : (lane + 1) * 128
                    ]
        return 0

    for g in range(groups):
        psi_copy(g).wait_recv()
        lax.fori_loop(g * (YB // groups), (g + 1) * (YB // groups), forward_z, 0)
    for s in range(PARTS):
        pcol_start(0, s, s1, r1)
    for load in loads[2:]:
        load.wait()
    for s in range(PARTS):
        block = jnp.concatenate([ker[s * K4 + m // 2] for m in range(8)], axis=0)
        weight[s] = jnp.concatenate([block, jnp.zeros((W, 64), F32)], axis=1).T[:N]

    def forward_y(s):
        pcol_wait(0, s, s1, r1)
        turned = jnp.concatenate([r1[s, lane].T for lane in range(3)], axis=0)
        spec = dot3(halves(turned), table(1), NN)
        spec = swap_slots([spec[m * XB : (m + 1) * XB] for m in range(8)])
        for w in range(8):
            s2[s, w // 2, (w % 2) * XB : (w % 2 + 1) * XB, :] = spec[w]
        prow_start(1, s, s2, r2)

    def middle_x(s):
        prow_wait(1, s, s2, r2)
        data = r2[s].reshape(W, W)
        freq = dot3(table(2), halves(data), NN)
        freq = jnp.concatenate([freq[:N] * weight[s], freq[N:] * weight[s]], axis=0)
        back = dot3(table(3), halves(freq), NN)
        s3[s] = back.reshape(PR, 2 * XB, W)
        prow_start(2, s, s3, r3)

    def backward_y(s):
        prow_wait(2, s, s3, r3)
        data = swap_slots([r3[s, w // 2, (w % 2) * XB : (w % 2 + 1) * XB, :] for w in range(8)])
        data = jnp.concatenate(data, axis=0)
        back = dot3(table(4), halves(data), NT)
        for lane in range(3):
            s4[s, lane] = back[:, lane * 128 : (lane + 1) * 128]
        pcol_start(3, s, s4, r4)

    forward_y(0)
    forward_y(1)
    middle_x(0)
    forward_y(2)
    middle_x(1)
    backward_y(0)
    middle_x(2)
    backward_y(1)
    backward_y(2)
    for s in range(PARTS):
        pcol_wait(3, s, s4, r4)

    def backward_z(y, _):
        near = jnp.concatenate(
            [
                jnp.concatenate([r4[s, lane, pl.ds(y * 2 + c, PC, stride=CH), :] for lane in range(3)], axis=1)
                for c in range(2)
                for s in range(PARTS)
            ],
            axis=0,
        )
        lhs = jnp.concatenate([near[:, k * 2 * XB : (k + 1) * 2 * XB] for k in range(K4)], axis=0)
        lhs = jnp.concatenate([lhs, jnp.zeros((W, 32), F32)], axis=1)
        field = dot3(halves(lhs.T[: 2 * XB]), table(5), NN)
        source = psi[pl.ds(pl.multiple_of(y * XB, 16), XB), :]
        for j in range(2):
            term = field[j * XB : (j + 1) * XB] * source
            rest = term[:, 256:]
            at = pl.ds(pl.multiple_of(y * XB, 16), XB)
            out_ref[j, at, :128] = term[:, :128] + term[:, 128:256]
            out_ref[j, at, 128:] = (rest + pltpu.roll(rest, 64, 1))[:, :64]
        return 0

    lax.fori_loop(0, YB, backward_z, 0)
    for g in range(groups):
        psi_copy(g).wait_send()
    for s in range(PARTS):
        pcol_sent(0, s, s1)
        prow_sent(1, s, s2)
        prow_sent(2, s, s3)
        pcol_sent(3, s, s4)


def spread(a):
    return jnp.concatenate([a[..., :128], a[..., :128], a[..., 128:], a[..., 128:]], axis=-1)


def on_device(orbitals, kernel, plan, occupation):
    orb = jnp.transpose(orbitals, (0, 2, 1, 3)).reshape(2, YB * XB, N)
    ker = jnp.transpose(kernel, (1, 0, 2))
    tables = jnp.asarray(np.stack(make_tables()))
    pcol_buf = pltpu.VMEM((PARTS, 3, PC * CH, 128), F32)
    prow_buf = pltpu.VMEM((PARTS, PR, 2 * XB, W), F32)
    vmem = pl.BlockSpec(memory_space=pltpu.VMEM)
    out = pl.pallas_call(
        body,
        out_shape=jax.ShapeDtypeStruct((2, YB * XB, N), F32),
        in_specs=[pl.BlockSpec(memory_space=pltpu.SMEM)] * 2 + [pl.BlockSpec(memory_space=pl.ANY)] * 3,
        out_specs=vmem,
        scratch_shapes=[
            pltpu.VMEM((2, YB * XB, N), F32),
            pltpu.VMEM((YB, XB, N), F32),
            pltpu.VMEM((PARTS, N, W), F32),
            pltpu.VMEM((12, W, W), BF16),
            pltpu.VMEM((YB * XB, W), F32),
            pltpu.VMEM((YB * XB, W), F32),
            pcol_buf, pcol_buf, prow_buf, prow_buf, prow_buf, prow_buf, pcol_buf, pcol_buf,
            pltpu.SemaphoreType.DMA((8,)),
            pltpu.SemaphoreType.DMA((3,)),
            pltpu.SemaphoreType.DMA((3,)),
            pltpu.SemaphoreType.DMA((4, PARTS)),
            pltpu.SemaphoreType.DMA((4, PARTS)),
            pltpu.SemaphoreType.DMA((4, PARTS)),
        ],
        compiler_params=pltpu.CompilerParams(
            collective_id=0, has_side_effects=True, vmem_limit_bytes=56 * 2**20
        ),
    )(plan, occupation, orb, ker, tables)
    return jnp.transpose(out.reshape(2, YB, XB, N), (0, 2, 1, 3))


def solution(mesh):
    return jax.shard_map(
        on_device,
        mesh=mesh,
        in_specs=(P("band", "prow", "pcol", None), P("prow", "pcol", None), P(), P()),
        out_specs=P("band", "prow", "pcol", None),
        check_vma=False,
    )
```

```python
import functools

import jax
import jax.numpy as jnp
import ml_dtypes
import numpy as np
from jax import lax
from jax.experimental import pallas as pl
from jax.experimental.pallas import tpu as pltpu
from jax.sharding import PartitionSpec as P

N = 192
PC = 16
PR = 4
YB = 12
XB = 48
PARTS = 3
K4 = 4
CUTS = 3
XC = 16
W = 384
CH = 24
F32 = jnp.float32
BF16 = jnp.bfloat16
MESH = pl.DeviceIdType.MESH


def split_table(table):
    high = table.astype(np.float32).astype(ml_dtypes.bfloat16)
    low = (table - high.astype(np.float64)).astype(np.float32).astype(ml_dtypes.bfloat16)
    return high, low


def complex_table(out_part, out_freq, in_part, in_point, sign):
    angle = 2.0 * np.pi * ((out_freq[:, None] * in_point[None, :]) % N) / N
    cosine, sine = np.cos(angle), sign * np.sin(angle)
    op, ip = out_part[:, None], in_part[None, :]
    return np.where(op == ip, cosine, np.where(op == 0, -sine, sine))


def grid(*sizes):
    return [a.reshape(-1) for a in np.meshgrid(*[np.arange(s) for s in sizes], indexing="ij")]


def make_tables():
    z_part = np.concatenate([np.zeros(128), np.ones(128), np.zeros(64), np.ones(64)]).astype(int)
    z_point = np.concatenate([np.arange(128)] * 2 + [np.arange(128, 192)] * 2)
    k4, c, s, q = grid(K4, 2, PARTS, PC)
    kz = q * YB + s * K4 + k4
    t1 = complex_table(c, kz, z_part, z_point, -1)
    t5 = -0.25 * complex_table(z_part, z_point, c, kz, 1).T
    p, y, yc = grid(PC, YB, 2)
    y_point = p * YB + y
    u, uc, k = grid(PR, 2, XB)
    ky = u * XB + k
    t2 = complex_table(uc, ky, yc, y_point, -1).T
    t4 = complex_table(yc, y_point, uc, ky, 1)
    xc, kx = grid(2, N)
    v, cut, vc, x = grid(PR, CUTS, 2, XC)
    x_point = v * XB + cut * XC + x
    t3 = complex_table(xc, kx, vc, x_point, -1)
    t3i = complex_table(vc, x_point, xc, kx, 1) / float(N) ** 3
    return [part for t in (t1, t2, t3, t3i, t4, t5) for part in split_table(t)]


def halves(x):
    high = x.astype(BF16)
    return high, (x - high.astype(F32)).astype(BF16)


def dot3(left, right, dims):
    def dot(a, b):
        return lax.dot_general(a, b, (dims, ((), ())), preferred_element_type=F32)

    return dot(left[0], right[0]) + (dot(left[0], right[1]) + dot(left[1], right[0]))


NN = ((1,), (0,))
NT = ((1,), (1,))


def swap_slots(blocks, width):
    count = len(blocks)
    lanes = count * width
    slot = lax.broadcasted_iota(jnp.int32, blocks[0].shape, 1) // width
    blocks = list(blocks)
    bit = 1
    while bit < count:
        keep = (slot & bit) == 0
        for m in range(count):
            if m & bit == 0:
                a, b = blocks[m], blocks[m + bit]
                blocks[m] = jnp.where(keep, a, pltpu.roll(b, width * bit, 1))
                blocks[m + bit] = jnp.where(keep, pltpu.roll(a, lanes - width * bit, 1), b)
        bit *= 2
    return blocks


def body(
    plan_ref, occ_ref, orb_hbm, ker_hbm, tables_hbm,
    out_ref,
    orb, ker, weight, tables, mine, other, psi, s1, r1, s2, r2, s3, r3, s4, r4,
    load_sem, psi_send, psi_recv, own_sem, send_sem, recv_sem,
):
    def table(t):
        return tables[2 * t], tables[2 * t + 1]

    me_p = lax.axis_index("pcol")
    me_r = lax.axis_index("prow")
    me_b = lax.axis_index("band")
    half = lax.rem(me_p // 2, 2)
    work = lax.rem(me_b + half, 2)
    partner = 1 - me_b

    barrier = pltpu.get_barrier_semaphore()

    def greet_p(k, _):
        to = lax.rem(me_p * 2 + me_b + k, 2 * PC)
        pl.semaphore_signal(
            barrier, inc=1, device_id={"pcol": to // 2, "band": lax.rem(to, 2)}, device_id_type=MESH
        )
        return 0

    def greet_r(k, _):
        pl.semaphore_signal(barrier, inc=1, device_id={"prow": lax.rem(me_r + k, PR)}, device_id_type=MESH)
        return 0

    loads = [
        pltpu.make_async_copy(orb_hbm.at[:, :, pl.ds(cut * XC, XC), :], orb.at[cut], load_sem.at[cut])
        for cut in range(CUTS)
    ]
    loads += [
        pltpu.make_async_copy(
            tables_hbm.at[pl.ds(2 * t, 2)], tables.at[pl.ds(2 * t, 2)], load_sem.at[4 + t]
        )
        for t in range(6)
    ]
    loads.append(pltpu.make_async_copy(ker_hbm, ker, load_sem.at[3]))
    for load in loads[: CUTS + 1]:
        load.start()
    lax.fori_loop(1, 2 * PC, greet_p, 0)
    lax.fori_loop(1, PR, greet_r, 0)

    rows = YB * XC

    def band_copy(cut):
        return pltpu.make_async_remote_copy(
            src_ref=mine.at[pl.ds(cut * rows, rows)],
            dst_ref=other.at[pl.ds(cut * rows, rows)],
            send_sem=psi_send.at[cut],
            recv_sem=psi_recv.at[cut],
            device_id={"band": partner},
            device_id_type=MESH,
        )

    for cut in range(CUTS):
        loads[cut].wait()
        for y in range(YB):
            at = pl.ds(cut * rows + y * XC, XC)
            mine[at, :128] = orb[cut, 0, y, :, :128]
            mine[at, 128:256] = orb[cut, 1, y, :, :128]
            mine[at, 256:] = jnp.concatenate([orb[cut, 0, y, :, 128:], orb[cut, 1, y, :, 128:]], axis=1)
        if cut == 0:
            pl.semaphore_wait(barrier, 2 * PC - 1 + PR - 1)
        band_copy(cut).start()
    for load in loads[CUTS + 1 :]:
        load.start()

    share = [
        [
            [
                jnp.where(
                    jnp.logical_and(plan_ref[r] == 2 * owner + t, occ_ref[2 * owner + t] != 0),
                    jnp.float32(1.0), jnp.float32(0.0),
                )
                for t in range(2)
            ]
            for owner in (me_b, partner)
        ]
        for r in range(2)
    ]
    first_half = lax.broadcasted_iota(jnp.int32, (XC, 128), 1) < 64
    straight = [jnp.where(first_half, share[0][g][0], share[1][g][1]) for g in range(2)]
    crossed = [jnp.where(first_half, share[0][g][1], share[1][g][0]) for g in range(2)]

    def pair_density(at):
        tiles = []
        for ref in (mine, other):
            high = ref[at, 256:]
            tiles.append((ref[at, :128], ref[at, 128:256], high, pltpu.roll(high, 64, 1)))
        source = [
            sum(share[r][g][t] * tiles[g][t] for g in range(2) for t in range(2)) for r in range(2)
        ]
        source.append(sum(straight[g] * tiles[g][2] + crossed[g] * tiles[g][3] for g in range(2)))
        for n in range(3):
            psi[at, n * 128 : (n + 1) * 128] = source[n]
        low0, low1, high, turned = [jnp.where(half == 1, b, a) for a, b in zip(*tiles)]
        phi = [(low0, jnp.where(first_half, high, turned)), (low1, jnp.where(first_half, turned, high))]
        return [
            jnp.concatenate([low * source[0], low * source[1], up * source[2]], axis=1) for low, up in phi
        ]

    def pcol_start(e, s, cut, src, dst):
        here = pl.ds(me_p * CH, CH)

        def send(k, _):
            to = lax.rem(me_p + k, PC)
            band = lax.rem(work + lax.rem(to // 2, 2), 2) if e == 0 else work
            pltpu.make_async_remote_copy(
                src_ref=src.at[s, cut, pl.ds(to * CH, CH), :],
                dst_ref=dst.at[s, cut, here, :],
                send_sem=send_sem.at[e, s, cut],
                recv_sem=recv_sem.at[e, s, cut],
                device_id={"pcol": to, "band": band},
                device_id_type=MESH,
            ).start()
            return 0

        own = pltpu.make_async_copy(src.at[s, cut, here, :], dst.at[s, cut, here, :], own_sem.at[e, s, cut])
        if e == 0:
            lax.fori_loop(1, PC, send, 0)
            own.start()
        else:
            lax.fori_loop(1 - half, PC, send, 0)
            pl.when(half == 0)(own.start)

    def pcol_all(sem, e, s, cut, ref):
        def wait_for(count):
            part = ref.at[s, cut, pl.ds(0, count * CH), :]
            return pltpu.make_async_copy(part, part, sem.at[e, s, cut]).wait

        if e == 0:
            wait_for(PC - 1)()
        else:
            pl.when(half == 0)(wait_for(PC - 1))
            pl.when(half == 1)(wait_for(PC))

    def pcol_wait(e, s, cut, src, dst):
        here = pl.ds(me_p * CH, CH)
        own = pltpu.make_async_copy(src.at[s, cut, here, :], dst.at[s, cut, here, :], own_sem.at[e, s, cut])
        if e == 0:
            own.wait()
        else:
            pl.when(half == 0)(own.wait)
        pcol_all(recv_sem, e, s, cut, dst)

    def pcol_sent(e, s, cut, src):
        pcol_all(send_sem, e, s, cut, src)

    def prow_start(e, s, cut, src, dst):
        def send(k, _):
            to = lax.rem(me_r + k, PR)
            pltpu.make_async_remote_copy(
                src_ref=src.at[s, to, cut],
                dst_ref=dst.at[s, me_r, cut],
                send_sem=send_sem.at[e, s, cut],
                recv_sem=recv_sem.at[e, s, cut],
                device_id={"prow": to},
                device_id_type=MESH,
            ).start()
            return 0

        lax.fori_loop(1, PR, send, 0)
        pltpu.make_async_copy(src.at[s, me_r, cut], dst.at[s, me_r, cut], own_sem.at[e, s, cut]).start()

    def prow_wait(e, s, cut, src, dst):
        pltpu.make_async_copy(src.at[s, me_r, cut], dst.at[s, me_r, cut], own_sem.at[e, s, cut]).wait()
        others = dst.at[s, pl.ds(0, PR - 1), cut]
        pltpu.make_async_copy(others, others, recv_sem.at[e, s, cut]).wait()

    def prow_sent(e, s, cut, src):
        others = src.at[s, pl.ds(0, PR - 1), cut]
        pltpu.make_async_copy(others, others, send_sem.at[e, s, cut]).wait()

    def forward_z(cut):
        def step(group, _):
            dens = []
            for y4 in range(4):
                y = group * 4 + y4
                dens += pair_density(pl.ds(pl.multiple_of(cut * rows + y * XC, 16), XC))
            spec = dot3(table(0), halves(jnp.concatenate(dens, axis=0)), NT)
            spec = swap_slots([spec[k * 96 : (k + 1) * 96] for k in range(K4)], 32)
            for y4 in range(4):
                for c in range(2):
                    for s in range(PARTS):
                        first = (c * PARTS + s) * PC
                        s1[s, cut, pl.ds((group * 4 + y4) * 2 + c, PC, stride=CH), :] = spec[y4][first : first + PC]
            return 0

        band_copy(cut).wait_recv()
        lax.fori_loop(0, YB // 4, step, 0)
        for s in range(PARTS):
            pcol_start(0, s, cut, s1, r1)

    def forward_y(parts, cut):
        for s in parts:
            pcol_wait(0, s, cut, s1, r1)
        turned = jnp.concatenate([r1[s, cut].T for s in parts], axis=0)
        spec = dot3(halves(turned), table(1), NN)
        for i, s in enumerate(parts):
            blocks = swap_slots([spec[i * 128 + m * XC : i * 128 + (m + 1) * XC] for m in range(8)], XB)
            for w in range(8):
                s2[s, w // 2, cut, (w % 2) * XC : (w % 2 + 1) * XC, :] = blocks[w]
            prow_start(1, s, cut, s2, r2)

    def middle_x(s):
        for cut in range(CUTS):
            prow_wait(1, s, cut, s2, r2)
        data = r2[s].reshape(W, W)
        freq = dot3(table(2), halves(data), NN)
        freq = jnp.concatenate([freq[:N] * weight[s], freq[N:] * weight[s]], axis=0)
        back = dot3(table(3), halves(freq), NN)
        s3[s] = back.reshape(PR, CUTS, 2 * XC, W)
        for cut in range(CUTS):
            prow_start(2, s, cut, s3, r3)

    def backward_y(s, cuts):
        data = []
        for cut in cuts:
            prow_wait(2, s, cut, s3, r3)
            data += swap_slots([r3[s, w // 2, cut, (w % 2) * XC : (w % 2 + 1) * XC, :] for w in range(8)], XB)
        back = dot3(table(4), halves(jnp.concatenate(data, axis=0)), NT)
        for i, cut in enumerate(cuts):
            s4[s, cut] = back[:, i * 128 : (i + 1) * 128]
            pcol_start(3, s, cut, s4, r4)

    def backward_z(cut):
        def step(group, _):
            near = [
                jnp.concatenate(
                    [
                        r4[s, cut, pl.ds((group * 4 + y4) * 2 + c, PC, stride=CH), :]
                        for c in range(2)
                        for s in range(PARTS)
                    ],
                    axis=0,
                )
                for y4 in range(4)
            ]
            near = jnp.concatenate(swap_slots(near, 32), axis=0)
            field = dot3(halves(near.T), table(5), NN)
            for y4 in range(4):
                y = group * 4 + y4
                source = psi[pl.ds(pl.multiple_of(cut * rows + y * XC, 16), XC), :]
                at = pl.ds(pl.multiple_of(y * XB + cut * XC, 16), XC)
                for j in range(2):
                    first = (y4 * 2 + j) * XC
                    term = field[first : first + XC] * source
                    rest = term[:, 256:]
                    out_ref[j, at, :128] = term[:, :128] + term[:, 128:256]
                    out_ref[j, at, 128:] = (rest + pltpu.roll(rest, 64, 1))[:, :64]
            return 0

        for s in range(PARTS):
            pcol_wait(3, s, cut, s4, r4)
        lax.fori_loop(0, YB // 4, step, 0)

    loads[CUTS].wait()
    forward_z(0)
    for load in loads[CUTS + 1 :]:
        load.wait()
    forward_z(1)
    for s in range(PARTS):
        block = jnp.concatenate([ker[s * K4 + m // 2] for m in range(8)], axis=0)
        weight[s] = jnp.concatenate([block, jnp.zeros((W, 64), F32)], axis=1).T[:N]
    forward_y((0, 1, 2), 0)
    forward_z(2)
    forward_y((0, 1, 2), 1)
    forward_y((0,), 2)
    forward_y((1,), 2)
    middle_x(0)
    forward_y((2,), 2)
    middle_x(1)
    backward_y(0, (0, 1, 2))
    middle_x(2)
    backward_y(1, (0, 1, 2))
    for cut in range(CUTS):
        backward_y(2, (cut,))
    for cut in range(CUTS):
        backward_z(cut)

    for cut in range(CUTS):
        band_copy(cut).wait_send()
        for s in range(PARTS):
            pcol_sent(0, s, cut, s1)
            prow_sent(1, s, cut, s2)
            prow_sent(2, s, cut, s3)
            pcol_sent(3, s, cut, s4)


def on_device(orbitals, kernel, plan, occupation):
    orb = jnp.transpose(orbitals, (0, 2, 1, 3))
    ker = jnp.transpose(kernel, (1, 0, 2))
    tables = jnp.asarray(np.stack(make_tables()))
    pcol_buf = pltpu.VMEM((PARTS, CUTS, PC * CH, 128), F32)
    prow_buf = pltpu.VMEM((PARTS, PR, CUTS, 2 * XC, W), F32)
    vmem = pl.BlockSpec(memory_space=pltpu.VMEM)
    out = pl.pallas_call(
        body,
        out_shape=jax.ShapeDtypeStruct((2, YB * XB, N), F32),
        in_specs=[pl.BlockSpec(memory_space=pltpu.SMEM)] * 2 + [pl.BlockSpec(memory_space=pl.ANY)] * 3,
        out_specs=vmem,
        scratch_shapes=[
            pltpu.VMEM((CUTS, 2, YB, XC, N), F32),
            pltpu.VMEM((YB, XB, N), F32),
            pltpu.VMEM((PARTS, N, W), F32),
            pltpu.VMEM((12, W, W), BF16),
            pltpu.VMEM((YB * XB, W), F32),
            pltpu.VMEM((YB * XB, W), F32),
            pltpu.VMEM((YB * XB, W), F32),
            pcol_buf, pcol_buf, prow_buf, prow_buf, prow_buf, prow_buf, pcol_buf, pcol_buf,
            pltpu.SemaphoreType.DMA((10,)),
            pltpu.SemaphoreType.DMA((3,)),
            pltpu.SemaphoreType.DMA((3,)),
            pltpu.SemaphoreType.DMA((4, PARTS, CUTS)),
            pltpu.SemaphoreType.DMA((4, PARTS, CUTS)),
            pltpu.SemaphoreType.DMA((4, PARTS, CUTS)),
        ],
        compiler_params=pltpu.CompilerParams(
            collective_id=0, has_side_effects=True, vmem_limit_bytes=56 * 2**20
        ),
    )(plan, occupation, orb, ker, tables)
    return jnp.transpose(out.reshape(2, YB, XB, N), (0, 2, 1, 3))


def solution(mesh):
    return jax.shard_map(
        on_device,
        mesh=mesh,
        in_specs=(P("band", "prow", "pcol", None), P("prow", "pcol", None), P(), P()),
        out_specs=P("band", "prow", "pcol", None),
        check_vma=False,
    )
```

```python
import functools

import jax
import jax.numpy as jnp
import ml_dtypes
import numpy as np
from jax import lax
from jax.experimental import pallas as pl
from jax.experimental.pallas import tpu as pltpu
from jax.sharding import PartitionSpec as P

N = 192
PC = 16
PR = 4
YB = 12
XB = 48
PARTS = 3
K4 = 4
CUTS = 3
XC = 16
W = 384
CH = 24
F32 = jnp.float32
BF16 = jnp.bfloat16
MESH = pl.DeviceIdType.MESH


def split_table(table):
    high = table.astype(np.float32).astype(ml_dtypes.bfloat16)
    low = (table - high.astype(np.float64)).astype(np.float32).astype(ml_dtypes.bfloat16)
    return high, low


def complex_table(out_part, out_freq, in_part, in_point, sign):
    angle = 2.0 * np.pi * ((out_freq[:, None] * in_point[None, :]) % N) / N
    cosine, sine = np.cos(angle), sign * np.sin(angle)
    op, ip = out_part[:, None], in_part[None, :]
    return np.where(op == ip, cosine, np.where(op == 0, -sine, sine))


def grid(*sizes):
    return [a.reshape(-1) for a in np.meshgrid(*[np.arange(s) for s in sizes], indexing="ij")]


def make_tables():
    z_part = np.concatenate([np.zeros(128), np.ones(128), np.zeros(64), np.ones(64)]).astype(int)
    z_point = np.concatenate([np.arange(128)] * 2 + [np.arange(128, 192)] * 2)
    k4, c, s, q = grid(K4, 2, PARTS, PC)
    kz = q * YB + s * K4 + k4
    t1 = complex_table(c, kz, z_part, z_point, -1)
    t5 = -0.25 * complex_table(z_part, z_point, c, kz, 1).T
    p, y, yc = grid(PC, YB, 2)
    y_point = p * YB + y
    u, uc, k = grid(PR, 2, XB)
    ky = u * XB + k
    t2 = complex_table(uc, ky, yc, y_point, -1).T
    t4 = complex_table(yc, y_point, uc, ky, 1)
    xc, kx = grid(2, N)
    v, cut, vc, x = grid(PR, CUTS, 2, XC)
    x_point = v * XB + cut * XC + x
    t3 = complex_table(xc, kx, vc, x_point, -1)
    t3i = complex_table(vc, x_point, xc, kx, 1) / float(N) ** 3
    return [part for t in (t1, t2, t3, t3i, t4, t5) for part in split_table(t)]


def halves(x):
    high = x.astype(BF16)
    return high, (x - high.astype(F32)).astype(BF16)


def dot3(left, right, dims):
    (left_dim,), (right_dim,) = dims
    long_left = jnp.concatenate([left[0], left[0], left[1]], axis=left_dim)
    long_right = jnp.concatenate([right[0], right[1], right[0]], axis=right_dim)
    return lax.dot_general(long_left, long_right, (dims, ((), ())), preferred_element_type=F32)


NN = ((1,), (0,))
NT = ((1,), (1,))


def swap_slots(blocks, width):
    count = len(blocks)
    lanes = count * width
    slot = lax.broadcasted_iota(jnp.int32, blocks[0].shape, 1) // width
    blocks = list(blocks)
    bit = 1
    while bit < count:
        keep = (slot & bit) == 0
        for m in range(count):
            if m & bit == 0:
                a, b = blocks[m], blocks[m + bit]
                blocks[m] = jnp.where(keep, a, pltpu.roll(b, width * bit, 1))
                blocks[m + bit] = jnp.where(keep, pltpu.roll(a, lanes - width * bit, 1), b)
        bit *= 2
    return blocks


def body(
    plan_ref, occ_ref, orb_hbm, ker_hbm, tables_hbm,
    out_ref,
    orb, ker, weight, tables, mine, other, psi, s1, r1, s2, r2, s3, r3, s4, r4,
    load_sem, psi_send, psi_recv, own_sem, send_sem, recv_sem,
):
    def table(t):
        return tables[2 * t], tables[2 * t + 1]

    me_p = lax.axis_index("pcol")
    me_r = lax.axis_index("prow")
    me_b = lax.axis_index("band")
    half = lax.rem(me_p // 2, 2)
    work = lax.rem(me_b + half, 2)
    partner = 1 - me_b

    barrier = pltpu.get_barrier_semaphore()

    def greet_p(k, _):
        to = lax.rem(me_p + k, PC)
        band = lax.rem(work + lax.rem(to // 2, 2), 2)
        pl.semaphore_signal(barrier, inc=1, device_id={"pcol": to, "band": band}, device_id_type=MESH)
        return 0

    def greet_r(k, _):
        pl.semaphore_signal(barrier, inc=1, device_id={"prow": lax.rem(me_r + k, PR)}, device_id_type=MESH)
        return 0

    loads = [
        pltpu.make_async_copy(orb_hbm.at[:, :, pl.ds(cut * XC, XC), :], orb.at[cut], load_sem.at[cut])
        for cut in range(CUTS)
    ]
    loads += [
        pltpu.make_async_copy(
            tables_hbm.at[pl.ds(2 * t, 2)], tables.at[pl.ds(2 * t, 2)], load_sem.at[4 + t]
        )
        for t in range(6)
    ]
    loads.append(pltpu.make_async_copy(ker_hbm, ker, load_sem.at[3]))
    for load in loads[: CUTS + 1]:
        load.start()
    pl.semaphore_signal(barrier, inc=1, device_id={"band": partner}, device_id_type=MESH)
    for k in range(1, PC):
        greet_p(k, 0)
    for k in range(1, PR):
        greet_r(k, 0)

    rows = YB * XC

    def band_copy(cut):
        return pltpu.make_async_remote_copy(
            src_ref=mine.at[pl.ds(cut * rows, rows)],
            dst_ref=other.at[pl.ds(cut * rows, rows)],
            send_sem=psi_send.at[cut],
            recv_sem=psi_recv.at[cut],
            device_id={"band": partner},
            device_id_type=MESH,
        )

    for cut in range(CUTS):
        loads[cut].wait()
        for y in range(YB):
            at = pl.ds(cut * rows + y * XC, XC)
            mine[at, :128] = orb[cut, 0, y, :, :128]
            mine[at, 128:256] = orb[cut, 1, y, :, :128]
            mine[at, 256:] = jnp.concatenate([orb[cut, 0, y, :, 128:], orb[cut, 1, y, :, 128:]], axis=1)
        if cut == 0:
            pl.semaphore_wait(barrier, 1 + PC - 1 + PR - 1)
        band_copy(cut).start()
    for load in loads[CUTS + 1 :]:
        load.start()

    share = [
        [
            [
                jnp.where(
                    jnp.logical_and(plan_ref[r] == 2 * owner + t, occ_ref[2 * owner + t] != 0),
                    jnp.float32(1.0), jnp.float32(0.0),
                )
                for t in range(2)
            ]
            for owner in (me_b, partner)
        ]
        for r in range(2)
    ]
    first_half = lax.broadcasted_iota(jnp.int32, (XC, 128), 1) < 64
    straight = [jnp.where(first_half, share[0][g][0], share[1][g][1]) for g in range(2)]
    crossed = [jnp.where(first_half, share[0][g][1], share[1][g][0]) for g in range(2)]

    def pair_density(at):
        tiles = []
        for ref in (mine, other):
            high = ref[at, 256:]
            tiles.append((ref[at, :128], ref[at, 128:256], high, pltpu.roll(high, 64, 1)))
        source = [
            sum(share[r][g][t] * tiles[g][t] for g in range(2) for t in range(2)) for r in range(2)
        ]
        source.append(sum(straight[g] * tiles[g][2] + crossed[g] * tiles[g][3] for g in range(2)))
        for n in range(3):
            psi[at, n * 128 : (n + 1) * 128] = source[n]
        low0, low1, high, turned = [jnp.where(half == 1, b, a) for a, b in zip(*tiles)]
        phi = [(low0, jnp.where(first_half, high, turned)), (low1, jnp.where(first_half, turned, high))]
        return [
            jnp.concatenate([low * source[0], low * source[1], up * source[2]], axis=1) for low, up in phi
        ]

    def pcol_start(e, s, cut, src, dst):
        here = pl.ds(me_p * CH, CH)

        def send(k, _):
            to = lax.rem(me_p + k, PC)
            band = lax.rem(work + lax.rem(to // 2, 2), 2) if e == 0 else work
            pltpu.make_async_remote_copy(
                src_ref=src.at[s, cut, pl.ds(to * CH, CH), :],
                dst_ref=dst.at[s, cut, here, :],
                send_sem=send_sem.at[e, s, cut],
                recv_sem=recv_sem.at[e, s, cut],
                device_id={"pcol": to, "band": band},
                device_id_type=MESH,
            ).start()
            return 0

        own = pltpu.make_async_copy(src.at[s, cut, here, :], dst.at[s, cut, here, :], own_sem.at[e, s, cut])
        if e == 0:
            lax.fori_loop(1, PC, send, 0)
            own.start()
        else:
            lax.fori_loop(1 - half, PC, send, 0)
            pl.when(half == 0)(own.start)

    def pcol_all(sem, e, s, cut, ref):
        def wait_for(count):
            part = ref.at[s, cut, pl.ds(0, count * CH), :]
            return pltpu.make_async_copy(part, part, sem.at[e, s, cut]).wait

        if e == 0:
            wait_for(PC - 1)()
        else:
            pl.when(half == 0)(wait_for(PC - 1))
            pl.when(half == 1)(wait_for(PC))

    def pcol_wait(e, s, cut, src, dst):
        here = pl.ds(me_p * CH, CH)
        own = pltpu.make_async_copy(src.at[s, cut, here, :], dst.at[s, cut, here, :], own_sem.at[e, s, cut])
        if e == 0:
            own.wait()
        else:
            pl.when(half == 0)(own.wait)
        pcol_all(recv_sem, e, s, cut, dst)

    def pcol_sent(e, s, cut, src):
        pcol_all(send_sem, e, s, cut, src)

    def prow_start(e, s, cut, src, dst):
        def send(k, _):
            to = lax.rem(me_r + k, PR)
            pltpu.make_async_remote_copy(
                src_ref=src.at[s, to, cut],
                dst_ref=dst.at[s, me_r, cut],
                send_sem=send_sem.at[e, s, cut],
                recv_sem=recv_sem.at[e, s, cut],
                device_id={"prow": to},
                device_id_type=MESH,
            ).start()
            return 0

        lax.fori_loop(1, PR, send, 0)
        pltpu.make_async_copy(src.at[s, me_r, cut], dst.at[s, me_r, cut], own_sem.at[e, s, cut]).start()

    def prow_wait(e, s, cut, src, dst):
        pltpu.make_async_copy(src.at[s, me_r, cut], dst.at[s, me_r, cut], own_sem.at[e, s, cut]).wait()
        others = dst.at[s, pl.ds(0, PR - 1), cut]
        pltpu.make_async_copy(others, others, recv_sem.at[e, s, cut]).wait()

    def prow_sent(e, s, cut, src):
        others = src.at[s, pl.ds(0, PR - 1), cut]
        pltpu.make_async_copy(others, others, send_sem.at[e, s, cut]).wait()

    def forward_z(cut):
        def step(group, _):
            dens = []
            for y4 in range(4):
                y = group * 4 + y4
                dens += pair_density(pl.ds(pl.multiple_of(cut * rows + y * XC, 16), XC))
            spec = dot3(table(0), halves(jnp.concatenate(dens, axis=0)), NT)
            spec = swap_slots([spec[k * 96 : (k + 1) * 96] for k in range(K4)], 32)
            for y4 in range(4):
                for c in range(2):
                    for s in range(PARTS):
                        first = (c * PARTS + s) * PC
                        s1[s, cut, pl.ds((group * 4 + y4) * 2 + c, PC, stride=CH), :] = spec[y4][first : first + PC]
            return 0

        band_copy(cut).wait_recv()
        lax.fori_loop(0, YB // 4, step, 0)

    def send_z(*which):
        for s, cut in which:
            pcol_start(0, s, cut, s1, r1)

    def forward_y(parts, cut):
        for s in parts:
            pcol_wait(0, s, cut, s1, r1)
        turned = jnp.concatenate([r1[s, cut].T for s in parts], axis=0)
        spec = dot3(halves(turned), table(1), NN)
        for i, s in enumerate(parts):
            blocks = swap_slots([spec[i * 128 + m * XC : i * 128 + (m + 1) * XC] for m in range(8)], XB)
            for w in range(8):
                s2[s, w // 2, cut, (w % 2) * XC : (w % 2 + 1) * XC, :] = blocks[w]
            prow_start(1, s, cut, s2, r2)

    def middle_x(s):
        for cut in range(CUTS):
            prow_wait(1, s, cut, s2, r2)
        data = r2[s].reshape(W, W)
        freq = dot3(table(2), halves(data), NN)
        freq = jnp.concatenate([freq[:N] * weight[s], freq[N:] * weight[s]], axis=0)
        back = dot3(table(3), halves(freq), NN)
        s3[s] = back.reshape(PR, CUTS, 2 * XC, W)
        for cut in range(CUTS):
            prow_start(2, s, cut, s3, r3)

    def backward_y(s, cuts):
        data = []
        for cut in cuts:
            prow_wait(2, s, cut, s3, r3)
            data += swap_slots([r3[s, w // 2, cut, (w % 2) * XC : (w % 2 + 1) * XC, :] for w in range(8)], XB)
        back = dot3(table(4), halves(jnp.concatenate(data, axis=0)), NT)
        for i, cut in enumerate(cuts):
            s4[s, cut] = back[:, i * 128 : (i + 1) * 128]
            pcol_start(3, s, cut, s4, r4)

    def backward_z(cut):
        def step(group, _):
            near = [
                jnp.concatenate(
                    [
                        r4[s, cut, pl.ds((group * 4 + y4) * 2 + c, PC, stride=CH), :]
                        for c in range(2)
                        for s in range(PARTS)
                    ],
                    axis=0,
                )
                for y4 in range(4)
            ]
            near = jnp.concatenate(swap_slots(near, 32), axis=0)
            field = dot3(halves(near.T), table(5), NN)
            for y4 in range(4):
                y = group * 4 + y4
                source = psi[pl.ds(pl.multiple_of(cut * rows + y * XC, 16), XC), :]
                at = pl.ds(pl.multiple_of(y * XB + cut * XC, 16), XC)
                for j in range(2):
                    first = (y4 * 2 + j) * XC
                    term = field[first : first + XC] * source
                    rest = term[:, 256:]
                    out_ref[j, at, :128] = term[:, :128] + term[:, 128:256]
                    out_ref[j, at, 128:] = (rest + pltpu.roll(rest, 64, 1))[:, :64]
            return 0

        for s in range(PARTS):
            pcol_wait(3, s, cut, s4, r4)
        lax.fori_loop(0, YB // 4, step, 0)

    loads[CUTS].wait()
    forward_z(0)
    send_z((0, 0), (1, 0), (2, 0))
    for load in loads[CUTS + 1 :]:
        load.wait()
    forward_z(1)
    send_z((0, 1), (1, 1), (2, 1))
    for s in range(PARTS):
        block = jnp.concatenate([ker[s * K4 + m // 2] for m in range(8)], axis=0)
        weight[s] = jnp.concatenate([block, jnp.zeros((W, 64), F32)], axis=1).T[:N]
    forward_y((0, 1, 2), 0)
    forward_z(2)
    send_z((0, 2), (1, 2), (2, 2))
    forward_y((0, 1, 2), 1)
    forward_y((0,), 2)
    forward_y((1,), 2)
    forward_y((2,), 2)
    middle_x(0)
    middle_x(1)
    middle_x(2)
    backward_y(0, (0, 1, 2))
    backward_y(1, (0, 1, 2))
    for cut in range(CUTS):
        backward_y(2, (cut,))
    for cut in range(CUTS):
        backward_z(cut)

    for cut in range(CUTS):
        band_copy(cut).wait_send()
        for s in range(PARTS):
            pcol_sent(0, s, cut, s1)
            prow_sent(1, s, cut, s2)
            prow_sent(2, s, cut, s3)
            pcol_sent(3, s, cut, s4)


def on_device(orbitals, kernel, plan, occupation):
    orb = jnp.transpose(orbitals, (0, 2, 1, 3))
    ker = jnp.transpose(kernel, (1, 0, 2))
    tables = jnp.asarray(np.stack(make_tables()))
    pcol_buf = pltpu.VMEM((PARTS, CUTS, PC * CH, 128), F32)
    prow_buf = pltpu.VMEM((PARTS, PR, CUTS, 2 * XC, W), F32)
    vmem = pl.BlockSpec(memory_space=pltpu.VMEM)
    out = pl.pallas_call(
        body,
        out_shape=jax.ShapeDtypeStruct((2, YB * XB, N), F32),
        in_specs=[pl.BlockSpec(memory_space=pltpu.SMEM)] * 2 + [pl.BlockSpec(memory_space=pl.ANY)] * 3,
        out_specs=vmem,
        scratch_shapes=[
            pltpu.VMEM((CUTS, 2, YB, XC, N), F32),
            pltpu.VMEM((YB, XB, N), F32),
            pltpu.VMEM((PARTS, N, W), F32),
            pltpu.VMEM((12, W, W), BF16),
            pltpu.VMEM((YB * XB, W), F32),
            pltpu.VMEM((YB * XB, W), F32),
            pltpu.VMEM((YB * XB, W), F32),
            pcol_buf, pcol_buf, prow_buf, prow_buf, prow_buf, prow_buf, pcol_buf, pcol_buf,
            pltpu.SemaphoreType.DMA((10,)),
            pltpu.SemaphoreType.DMA((3,)),
            pltpu.SemaphoreType.DMA((3,)),
            pltpu.SemaphoreType.DMA((4, PARTS, CUTS)),
            pltpu.SemaphoreType.DMA((4, PARTS, CUTS)),
            pltpu.SemaphoreType.DMA((4, PARTS, CUTS)),
        ],
        compiler_params=pltpu.CompilerParams(
            collective_id=0, has_side_effects=True, vmem_limit_bytes=56 * 2**20
        ),
    )(plan, occupation, orb, ker, tables)
    return jnp.transpose(out.reshape(2, YB, XB, N), (0, 2, 1, 3))


def solution(mesh):
    return jax.shard_map(
        on_device,
        mesh=mesh,
        in_specs=(P("band", "prow", "pcol", None), P("prow", "pcol", None), P(), P()),
        out_specs=P("band", "prow", "pcol", None),
        check_vma=False,
    )
```

```python
import functools

import jax
import jax.numpy as jnp
import ml_dtypes
import numpy as np
from jax import lax
from jax.experimental import pallas as pl
from jax.experimental.pallas import tpu as pltpu
from jax.sharding import PartitionSpec as P

N = 192
PC = 16
PR = 4
YB = 12
XB = 48
PARTS = 3
K4 = 4
CUTS = 3
XC = 16
BAND_PIECES = (3, 3, 3)
W = 384
CH = 24
F32 = jnp.float32
BF16 = jnp.bfloat16
MESH = pl.DeviceIdType.MESH


def split_table(table):
    high = table.astype(np.float32).astype(ml_dtypes.bfloat16)
    low = (table - high.astype(np.float64)).astype(np.float32).astype(ml_dtypes.bfloat16)
    return high, low


def complex_table(out_part, out_freq, in_part, in_point, sign):
    angle = 2.0 * np.pi * ((out_freq[:, None] * in_point[None, :]) % N) / N
    cosine, sine = np.cos(angle), sign * np.sin(angle)
    op, ip = out_part[:, None], in_part[None, :]
    return np.where(op == ip, cosine, np.where(op == 0, -sine, sine))


def grid(*sizes):
    return [a.reshape(-1) for a in np.meshgrid(*[np.arange(s) for s in sizes], indexing="ij")]


def make_tables():
    z_part = np.concatenate([np.zeros(128), np.ones(128), np.zeros(64), np.ones(64)]).astype(int)
    z_point = np.concatenate([np.arange(128)] * 2 + [np.arange(128, 192)] * 2)
    k4, c, s, q = grid(K4, 2, PARTS, PC)
    kz = q * YB + s * K4 + k4
    t1 = complex_table(c, kz, z_part, z_point, -1)
    t5 = -0.25 * complex_table(z_part, z_point, c, kz, 1).T
    p, y, yc = grid(PC, YB, 2)
    y_point = p * YB + y
    u, uc, k = grid(PR, 2, XB)
    ky = u * XB + k
    t2 = complex_table(uc, ky, yc, y_point, -1).T
    t4 = complex_table(yc, y_point, uc, ky, 1)
    xc, kx = grid(2, N)
    v, cut, vc, x = grid(PR, CUTS, 2, XC)
    x_point = v * XB + cut * XC + x
    t3 = complex_table(xc, kx, vc, x_point, -1)
    t3i = complex_table(vc, x_point, xc, kx, 1) / float(N) ** 3
    return [part for t in (t1, t2, t3, t3i, t4, t5) for part in split_table(t)]


def halves(x):
    high = x.astype(BF16)
    return high, (x - high.astype(F32)).astype(BF16)


def dot3(left, right, dims):
    (left_dim,), (right_dim,) = dims
    long_left = jnp.concatenate([left[0], left[0], left[1]], axis=left_dim)
    long_right = jnp.concatenate([right[0], right[1], right[0]], axis=right_dim)
    return lax.dot_general(long_left, long_right, (dims, ((), ())), preferred_element_type=F32)


NN = ((1,), (0,))
NT = ((1,), (1,))


def swap_slots(blocks, width):
    count = len(blocks)
    lanes = count * width
    slot = lax.broadcasted_iota(jnp.int32, blocks[0].shape, 1) // width
    blocks = list(blocks)
    bit = 1
    while bit < count:
        keep = (slot & bit) == 0
        for m in range(count):
            if m & bit == 0:
                a, b = blocks[m], blocks[m + bit]
                blocks[m] = jnp.where(keep, a, pltpu.roll(b, width * bit, 1))
                blocks[m + bit] = jnp.where(keep, pltpu.roll(a, lanes - width * bit, 1), b)
        bit *= 2
    return blocks


def body(
    plan_ref, occ_ref, orb_hbm, ker_hbm, tables_hbm,
    out_ref,
    orb, ker, weight, tables, mine, other, psi, s1, r1, s2, r2, s3, r3, s4, r4,
    load_sem, pcol_sems, psi_send, psi_recv, own_sem, send_sem, recv_sem,
):
    def table(t):
        return tables[2 * t], tables[2 * t + 1]

    me_p = lax.axis_index("pcol")
    me_r = lax.axis_index("prow")
    me_b = lax.axis_index("band")
    half = lax.rem(me_p // 2, 2)
    work = lax.rem(me_b + half, 2)
    partner = 1 - me_b

    barrier = pltpu.get_barrier_semaphore()

    def greet_p(k, _):
        to = lax.rem(me_p + k, PC)
        band = lax.rem(work + lax.rem(to // 2, 2), 2)
        pl.semaphore_signal(barrier, inc=1, device_id={"pcol": to, "band": band}, device_id_type=MESH)
        return 0

    def greet_r(k, _):
        pl.semaphore_signal(barrier, inc=1, device_id={"prow": lax.rem(me_r + k, PR)}, device_id_type=MESH)
        return 0

    loads = [
        pltpu.make_async_copy(orb_hbm.at[:, :, pl.ds(cut * XC, XC), :], orb.at[cut], load_sem.at[cut])
        for cut in range(CUTS)
    ]
    loads += [
        pltpu.make_async_copy(
            tables_hbm.at[pl.ds(2 * t, 2)], tables.at[pl.ds(2 * t, 2)], load_sem.at[4 + t]
        )
        for t in range(6)
    ]
    loads.append(pltpu.make_async_copy(ker_hbm, ker, load_sem.at[3]))
    for load in loads[: CUTS + 1]:
        load.start()
    pl.semaphore_signal(barrier, inc=1, device_id={"band": partner}, device_id_type=MESH)
    for k in range(1, PC):
        greet_p(k, 0)
    for k in range(1, PR):
        greet_r(k, 0)

    rows = YB * XC

    def band_copy(cut, piece):
        size = rows // BAND_PIECES[cut]
        at = pl.ds(cut * rows + piece * size, size)
        return pltpu.make_async_remote_copy(
            src_ref=mine.at[at],
            dst_ref=other.at[at],
            send_sem=psi_send.at[cut, piece],
            recv_sem=psi_recv.at[cut, piece],
            device_id={"band": partner},
            device_id_type=MESH,
        )

    for cut in range(CUTS):
        loads[cut].wait()
        for y in range(YB):
            at = pl.ds(cut * rows + y * XC, XC)
            mine[at, :128] = orb[cut, 0, y, :, :128]
            mine[at, 128:256] = orb[cut, 1, y, :, :128]
            mine[at, 256:] = jnp.concatenate([orb[cut, 0, y, :, 128:], orb[cut, 1, y, :, 128:]], axis=1)
            if cut == 0 and y == YB // BAND_PIECES[0] - 1:
                pl.semaphore_wait(barrier, 1 + PC - 1 + PR - 1)
            if (y + 1) % (YB // BAND_PIECES[cut]) == 0:
                band_copy(cut, (y + 1) // (YB // BAND_PIECES[cut]) - 1).start()
    for load in loads[CUTS + 1 :]:
        load.start()

    share = [
        [
            [
                jnp.where(
                    jnp.logical_and(plan_ref[r] == 2 * owner + t, occ_ref[2 * owner + t] != 0),
                    jnp.float32(1.0), jnp.float32(0.0),
                )
                for t in range(2)
            ]
            for owner in (me_b, partner)
        ]
        for r in range(2)
    ]
    first_half = lax.broadcasted_iota(jnp.int32, (XC, 128), 1) < 64
    straight = [jnp.where(first_half, share[0][g][0], share[1][g][1]) for g in range(2)]
    crossed = [jnp.where(first_half, share[0][g][1], share[1][g][0]) for g in range(2)]

    def pair_density(at):
        tiles = []
        for ref in (mine, other):
            high = ref[at, 256:]
            tiles.append((ref[at, :128], ref[at, 128:256], high, pltpu.roll(high, 64, 1)))
        source = [
            sum(share[r][g][t] * tiles[g][t] for g in range(2) for t in range(2)) for r in range(2)
        ]
        source.append(sum(straight[g] * tiles[g][2] + crossed[g] * tiles[g][3] for g in range(2)))
        for n in range(3):
            psi[at, n * 128 : (n + 1) * 128] = source[n]
        low0, low1, high, turned = [jnp.where(half == 1, b, a) for a, b in zip(*tiles)]
        phi = [(low0, jnp.where(first_half, high, turned)), (low1, jnp.where(first_half, turned, high))]
        return [
            jnp.concatenate([low * source[0], low * source[1], up * source[2]], axis=1) for low, up in phi
        ]

    numbers = {}

    def pcol_at(ref, bundle, owner, count=1):
        s, parts, cut, cuts, y, ys = bundle
        first, size = (owner * CH + 2 * y, 2 * ys) if count == 1 else (0, 2 * ys * count)
        return ref.at[pl.ds(s, parts), pl.ds(cut, cuts), pl.ds(first, size), :]

    def pcol_own(e, bundle, src, dst):
        sem = pcol_sems.at[2, numbers[e, bundle]]
        return pltpu.make_async_copy(pcol_at(src, bundle, me_p), pcol_at(dst, bundle, me_p), sem)

    def pcol_start(e, bundle, src, dst):
        number = numbers.setdefault((e, bundle), len(numbers))

        def send(k, _):
            to = lax.rem(me_p + k, PC)
            band = lax.rem(work + lax.rem(to // 2, 2), 2) if e == 0 else work
            pltpu.make_async_remote_copy(
                src_ref=pcol_at(src, bundle, to),
                dst_ref=pcol_at(dst, bundle, me_p),
                send_sem=pcol_sems.at[0, number],
                recv_sem=pcol_sems.at[1, number],
                device_id={"pcol": to, "band": band},
                device_id_type=MESH,
            ).start()
            return 0

        own = pcol_own(e, bundle, src, dst)
        if e == 0:
            for k in range(1, PC):
                send(k, 0)
            own.start()
        else:
            lax.fori_loop(1 - half, PC, send, 0)
            pl.when(half == 0)(own.start)

    def pcol_all(which, e, bundle, ref):
        def wait_for(count):
            part = pcol_at(ref, bundle, 0, count)
            return pltpu.make_async_copy(part, part, pcol_sems.at[which, numbers[e, bundle]]).wait

        if e == 0:
            wait_for(PC - 1)()
        else:
            pl.when(half == 0)(wait_for(PC - 1))
            pl.when(half == 1)(wait_for(PC))

    waited = set()

    def pcol_wait(e, bundle, src, dst):
        if (e, bundle) in waited:
            return
        waited.add((e, bundle))
        own = pcol_own(e, bundle, src, dst)
        if e == 0:
            own.wait()
        else:
            pl.when(half == 0)(own.wait)
        pcol_all(1, e, bundle, dst)

    def pcol_sent(e, bundle, src):
        pcol_all(0, e, bundle, src)

    Y_PIECES = (3, 3, 3)

    def forward_bundles(s, cut):
        if cut < len(Y_PIECES):
            return [(0, PARTS, cut, 1, y, YB // Y_PIECES[cut]) for y in range(0, YB, YB // Y_PIECES[cut])]
        return [(s, 1, cut, 1, 0, YB)]

    def back_bundle(s, cut):
        return (s, 1, 0, CUTS, 0, YB) if s < 0 else (s, 1, cut, 1, 0, YB)

    def prow_start(e, s, cut, src, dst):
        def send(k, _):
            to = lax.rem(me_r + k, PR)
            pltpu.make_async_remote_copy(
                src_ref=src.at[s, to, cut],
                dst_ref=dst.at[s, me_r, cut],
                send_sem=send_sem.at[e, s, cut],
                recv_sem=recv_sem.at[e, s, cut],
                device_id={"prow": to},
                device_id_type=MESH,
            ).start()
            return 0

        lax.fori_loop(1, PR, send, 0)
        pltpu.make_async_copy(src.at[s, me_r, cut], dst.at[s, me_r, cut], own_sem.at[e, s, cut]).start()

    def prow_wait(e, s, cut, src, dst):
        pltpu.make_async_copy(src.at[s, me_r, cut], dst.at[s, me_r, cut], own_sem.at[e, s, cut]).wait()
        others = dst.at[s, pl.ds(0, PR - 1), cut]
        pltpu.make_async_copy(others, others, recv_sem.at[e, s, cut]).wait()

    def prow_sent(e, s, cut, src):
        others = src.at[s, pl.ds(0, PR - 1), cut]
        pltpu.make_async_copy(others, others, send_sem.at[e, s, cut]).wait()

    def forward_z(cut):
        def step(group, _):
            dens = []
            for y4 in range(4):
                y = group * 4 + y4
                dens += pair_density(pl.ds(pl.multiple_of(cut * rows + y * XC, 16), XC))
            spec = dot3(table(0), halves(jnp.concatenate(dens, axis=0)), NT)
            spec = swap_slots([spec[k * 96 : (k + 1) * 96] for k in range(K4)], 32)
            for y4 in range(4):
                for c in range(2):
                    for s in range(PARTS):
                        first = (c * PARTS + s) * PC
                        s1[s, cut, pl.ds((group * 4 + y4) * 2 + c, PC, stride=CH), :] = spec[y4][first : first + PC]
            return 0

        for piece in range(BAND_PIECES[cut]):
            band_copy(cut, piece).wait_recv()
            groups = YB // 4 // BAND_PIECES[cut]
            lax.fori_loop(piece * groups, (piece + 1) * groups, step, 0)
            for s in range(PARTS):
                for bundle in forward_bundles(s, cut):
                    ready = (piece + 1) * groups * 4
                    if bundle[4] + bundle[5] <= ready and (0, bundle) not in numbers:
                        pcol_start(0, bundle, s1, r1)

    def forward_y(parts, cut):
        for s in parts:
            for bundle in forward_bundles(s, cut):
                pcol_wait(0, bundle, s1, r1)
        turned = jnp.concatenate([r1[s, cut].T for s in parts], axis=0)
        spec = dot3(halves(turned), table(1), NN)
        for i, s in enumerate(parts):
            blocks = swap_slots([spec[i * 128 + m * XC : i * 128 + (m + 1) * XC] for m in range(8)], XB)
            for w in range(8):
                s2[s, w // 2, cut, (w % 2) * XC : (w % 2 + 1) * XC, :] = blocks[w]
            prow_start(1, s, cut, s2, r2)

    def middle_x(s):
        for cut in range(CUTS):
            prow_wait(1, s, cut, s2, r2)
        data = r2[s].reshape(W, W)
        freq = dot3(table(2), halves(data), NN)
        freq = jnp.concatenate([freq[:N] * weight[s], freq[N:] * weight[s]], axis=0)
        back = dot3(table(3), halves(freq), NN)
        s3[s] = back.reshape(PR, CUTS, 2 * XC, W)
        for cut in range(CUTS):
            prow_start(2, s, cut, s3, r3)

    def backward_y(s, cuts):
        data = []
        for cut in cuts:
            prow_wait(2, s, cut, s3, r3)
            data += swap_slots([r3[s, w // 2, cut, (w % 2) * XC : (w % 2 + 1) * XC, :] for w in range(8)], XB)
        back = dot3(table(4), halves(jnp.concatenate(data, axis=0)), NT)
        for i, cut in enumerate(cuts):
            s4[s, cut] = back[:, i * 128 : (i + 1) * 128]
            if cut == CUTS - 1 or back_bundle(s, cut) != back_bundle(s, cut + 1):
                pcol_start(3, back_bundle(s, cut), s4, r4)

    def backward_z(cut):
        def step(group, _):
            near = [
                jnp.concatenate(
                    [
                        r4[s, cut, pl.ds((group * 4 + y4) * 2 + c, PC, stride=CH), :]
                        for c in range(2)
                        for s in range(PARTS)
                    ],
                    axis=0,
                )
                for y4 in range(4)
            ]
            near = jnp.concatenate(swap_slots(near, 32), axis=0)
            field = dot3(halves(near.T), table(5), NN)
            for y4 in range(4):
                y = group * 4 + y4
                source = psi[pl.ds(pl.multiple_of(cut * rows + y * XC, 16), XC), :]
                at = pl.ds(pl.multiple_of(y * XB + cut * XC, 16), XC)
                for j in range(2):
                    first = (y4 * 2 + j) * XC
                    term = field[first : first + XC] * source
                    rest = term[:, 256:]
                    out_ref[j, at, :128] = term[:, :128] + term[:, 128:256]
                    out_ref[j, at, 128:] = (rest + pltpu.roll(rest, 64, 1))[:, :64]
            return 0

        for s in range(PARTS):
            pcol_wait(3, back_bundle(s, cut), s4, r4)
        lax.fori_loop(0, YB // 4, step, 0)

    loads[CUTS].wait()
    forward_z(0)
    for load in loads[CUTS + 1 :]:
        load.wait()
    forward_z(1)
    for s in range(PARTS):
        block = jnp.concatenate([ker[s * K4 + m // 2] for m in range(8)], axis=0)
        weight[s] = jnp.concatenate([block, jnp.zeros((W, 64), F32)], axis=1).T[:N]
    forward_y((0, 1, 2), 0)
    forward_z(2)
    forward_y((0, 1, 2), 1)
    forward_y((0,), 2)
    forward_y((1,), 2)
    forward_y((2,), 2)
    middle_x(0)
    middle_x(1)
    middle_x(2)
    for part in (0, 1):
        for cut in range(CUTS):
            backward_y(part, (cut,))
    for cut in range(CUTS):
        backward_y(2, (cut,))
    for cut in range(CUTS):
        backward_z(cut)

    for cut in range(CUTS):
        for piece in range(BAND_PIECES[cut]):
            band_copy(cut, piece).wait_send()
        for s in range(PARTS):
            prow_sent(1, s, cut, s2)
            prow_sent(2, s, cut, s3)
    for e, bundle in numbers:
        pcol_sent(e, bundle, s1 if e == 0 else s4)


def on_device(orbitals, kernel, plan, occupation):
    orb = jnp.transpose(orbitals, (0, 2, 1, 3))
    ker = jnp.transpose(kernel, (1, 0, 2))
    tables = jnp.asarray(np.stack(make_tables()))
    pcol_buf = pltpu.VMEM((PARTS, CUTS, PC * CH, 128), F32)
    prow_buf = pltpu.VMEM((PARTS, PR, CUTS, 2 * XC, W), F32)
    vmem = pl.BlockSpec(memory_space=pltpu.VMEM)
    out = pl.pallas_call(
        body,
        out_shape=jax.ShapeDtypeStruct((2, YB * XB, N), F32),
        in_specs=[pl.BlockSpec(memory_space=pltpu.SMEM)] * 2 + [pl.BlockSpec(memory_space=pl.ANY)] * 3,
        out_specs=vmem,
        scratch_shapes=[
            pltpu.VMEM((CUTS, 2, YB, XC, N), F32),
            pltpu.VMEM((YB, XB, N), F32),
            pltpu.VMEM((PARTS, N, W), F32),
            pltpu.VMEM((12, W, W), BF16),
            pltpu.VMEM((YB * XB, W), F32),
            pltpu.VMEM((YB * XB, W), F32),
            pltpu.VMEM((YB * XB, W), F32),
            pcol_buf, pcol_buf, prow_buf, prow_buf, prow_buf, prow_buf, pcol_buf, pcol_buf,
            pltpu.SemaphoreType.DMA((10,)),
            pltpu.SemaphoreType.DMA((3, 24)),
            pltpu.SemaphoreType.DMA((CUTS, 3)),
            pltpu.SemaphoreType.DMA((CUTS, 3)),
            pltpu.SemaphoreType.DMA((4, PARTS, CUTS)),
            pltpu.SemaphoreType.DMA((4, PARTS, CUTS)),
            pltpu.SemaphoreType.DMA((4, PARTS, CUTS)),
        ],
        compiler_params=pltpu.CompilerParams(
            collective_id=0, has_side_effects=True, vmem_limit_bytes=56 * 2**20
        ),
    )(plan, occupation, orb, ker, tables)
    return jnp.transpose(out.reshape(2, YB, XB, N), (0, 2, 1, 3))


def solution(mesh):
    return jax.shard_map(
        on_device,
        mesh=mesh,
        in_specs=(P("band", "prow", "pcol", None), P("prow", "pcol", None), P(), P()),
        out_specs=P("band", "prow", "pcol", None),
        check_vma=False,
    )
```

```python
import functools

import jax
import jax.numpy as jnp
import ml_dtypes
import numpy as np
from jax import lax
from jax.experimental import pallas as pl
from jax.experimental.pallas import tpu as pltpu
from jax.sharding import PartitionSpec as P

N = 192
PC = 16
PR = 4
YB = 12
XB = 48
PARTS = 3
K4 = 4
CUTS = 3
XC = 16
BAND_PIECES = (3, 3, 3)
W = 384
CH = 24
F32 = jnp.float32
BF16 = jnp.bfloat16
MESH = pl.DeviceIdType.MESH


def split_table(table):
    high = table.astype(np.float32).astype(ml_dtypes.bfloat16)
    low = (table - high.astype(np.float64)).astype(np.float32).astype(ml_dtypes.bfloat16)
    return high, low


def complex_table(out_part, out_freq, in_part, in_point, sign):
    angle = 2.0 * np.pi * ((out_freq[:, None] * in_point[None, :]) % N) / N
    cosine, sine = np.cos(angle), sign * np.sin(angle)
    op, ip = out_part[:, None], in_part[None, :]
    return np.where(op == ip, cosine, np.where(op == 0, -sine, sine))


def grid(*sizes):
    return [a.reshape(-1) for a in np.meshgrid(*[np.arange(s) for s in sizes], indexing="ij")]


def make_tables():
    z_part = np.concatenate([np.zeros(128), np.ones(128), np.zeros(64), np.ones(64)]).astype(int)
    z_point = np.concatenate([np.arange(128)] * 2 + [np.arange(128, 192)] * 2)
    k4, c, s, q = grid(K4, 2, PARTS, PC)
    kz = q * YB + s * K4 + k4
    t1 = complex_table(c, kz, z_part, z_point, -1)
    t5 = -0.25 * complex_table(z_part, z_point, c, kz, 1).T
    p, y, yc = grid(PC, YB, 2)
    y_point = p * YB + y
    u, uc, k = grid(PR, 2, XB)
    ky = u * XB + k
    t2 = complex_table(uc, ky, yc, y_point, -1).T
    t4 = complex_table(yc, y_point, uc, ky, 1)
    xc, kx = grid(2, N)
    v, cut, vc, x = grid(PR, CUTS, 2, XC)
    x_point = v * XB + cut * XC + x
    t3 = complex_table(xc, kx, vc, x_point, -1)
    t3i = complex_table(vc, x_point, xc, kx, 1) / float(N) ** 3
    return [part for t in (t1, t2, t3, t3i, t4, t5) for part in split_table(t)]


def halves(x):
    high = x.astype(BF16)
    return high, (x - high.astype(F32)).astype(BF16)


def dot3(left, right, dims):
    (left_dim,), (right_dim,) = dims
    long_left = jnp.concatenate([left[0], left[0], left[1]], axis=left_dim)
    long_right = jnp.concatenate([right[0], right[1], right[0]], axis=right_dim)
    return lax.dot_general(long_left, long_right, (dims, ((), ())), preferred_element_type=F32)


NN = ((1,), (0,))
NT = ((1,), (1,))


def swap_slots(blocks, width):
    count = len(blocks)
    lanes = count * width
    slot = lax.broadcasted_iota(jnp.int32, blocks[0].shape, 1) // width
    blocks = list(blocks)
    bit = 1
    while bit < count:
        keep = (slot & bit) == 0
        for m in range(count):
            if m & bit == 0:
                a, b = blocks[m], blocks[m + bit]
                blocks[m] = jnp.where(keep, a, pltpu.roll(b, width * bit, 1))
                blocks[m + bit] = jnp.where(keep, pltpu.roll(a, lanes - width * bit, 1), b)
        bit *= 2
    return blocks


def body(
    plan_ref, occ_ref, orb_hbm, ker_hbm, tables_hbm,
    out_ref,
    orb, ker, weight, tables, mine, other, psi, s1, r1, s2, r2, s3, r3, s4, r4,
    load_sem, pcol_sems, psi_send, psi_recv, own_sem, send_sem, recv_sem,
):
    def table(t):
        return tables[2 * t], tables[2 * t + 1]

    me_p = lax.axis_index("pcol")
    me_r = lax.axis_index("prow")
    me_b = lax.axis_index("band")
    half = lax.rem(me_p // 2, 2)
    work = lax.rem(me_b + half, 2)
    partner = 1 - me_b

    barrier = pltpu.get_barrier_semaphore()

    def greet_p(k, _):
        to = lax.rem(me_p + k, PC)
        band = lax.rem(work + lax.rem(to // 2, 2), 2)
        pl.semaphore_signal(barrier, inc=1, device_id={"pcol": to, "band": band}, device_id_type=MESH)
        return 0

    def greet_r(k, _):
        pl.semaphore_signal(barrier, inc=1, device_id={"prow": lax.rem(me_r + k, PR)}, device_id_type=MESH)
        return 0

    loads = [
        pltpu.make_async_copy(orb_hbm.at[:, :, pl.ds(cut * XC, XC), :], orb.at[cut], load_sem.at[cut])
        for cut in range(CUTS)
    ]
    loads += [
        pltpu.make_async_copy(
            tables_hbm.at[pl.ds(2 * t, 2)], tables.at[pl.ds(2 * t, 2)], load_sem.at[4 + t]
        )
        for t in range(6)
    ]
    loads.append(pltpu.make_async_copy(ker_hbm, ker, load_sem.at[3]))
    loads[0].start()
    pl.semaphore_signal(barrier, inc=1, device_id={"band": partner}, device_id_type=MESH)
    for k in range(1, PC):
        greet_p(k, 0)
    for k in range(1, PR):
        greet_r(k, 0)

    for load in loads[1 : CUTS + 1]:
        load.start()
    rows = YB * XC

    def band_copy(cut, piece):
        size = rows // BAND_PIECES[cut]
        at = pl.ds(cut * rows + piece * size, size)
        return pltpu.make_async_remote_copy(
            src_ref=mine.at[at],
            dst_ref=other.at[at],
            send_sem=psi_send.at[cut, piece],
            recv_sem=psi_recv.at[cut, piece],
            device_id={"band": partner},
            device_id_type=MESH,
        )

    for cut in range(CUTS):
        loads[cut].wait()
        for y in range(YB):
            at = pl.ds(cut * rows + y * XC, XC)
            mine[at, :128] = orb[cut, 0, y, :, :128]
            mine[at, 128:256] = orb[cut, 1, y, :, :128]
            mine[at, 256:] = jnp.concatenate([orb[cut, 0, y, :, 128:], orb[cut, 1, y, :, 128:]], axis=1)
            if cut == 0 and y == YB // BAND_PIECES[0] - 1:
                pl.semaphore_wait(barrier, 1 + PC - 1 + PR - 1)
            if (y + 1) % (YB // BAND_PIECES[cut]) == 0:
                band_copy(cut, (y + 1) // (YB // BAND_PIECES[cut]) - 1).start()
    for load in loads[CUTS + 1 :]:
        load.start()

    share = [
        [
            [
                jnp.where(
                    jnp.logical_and(plan_ref[r] == 2 * owner + t, occ_ref[2 * owner + t] != 0),
                    jnp.float32(1.0), jnp.float32(0.0),
                )
                for t in range(2)
            ]
            for owner in (me_b, partner)
        ]
        for r in range(2)
    ]
    first_half = lax.broadcasted_iota(jnp.int32, (XC, 128), 1) < 64
    straight = [jnp.where(first_half, share[0][g][0], share[1][g][1]) for g in range(2)]
    crossed = [jnp.where(first_half, share[0][g][1], share[1][g][0]) for g in range(2)]

    def pair_density(at):
        tiles = []
        for ref in (mine, other):
            high = ref[at, 256:]
            tiles.append((ref[at, :128], ref[at, 128:256], high, pltpu.roll(high, 64, 1)))
        source = [
            sum(share[r][g][t] * tiles[g][t] for g in range(2) for t in range(2)) for r in range(2)
        ]
        source.append(sum(straight[g] * tiles[g][2] + crossed[g] * tiles[g][3] for g in range(2)))
        for n in range(3):
            psi[at, n * 128 : (n + 1) * 128] = source[n]
        low0, low1, high, turned = [jnp.where(half == 1, b, a) for a, b in zip(*tiles)]
        phi = [(low0, jnp.where(first_half, high, turned)), (low1, jnp.where(first_half, turned, high))]
        return [
            jnp.concatenate([low * source[0], low * source[1], up * source[2]], axis=1) for low, up in phi
        ]

    numbers = {}

    def pcol_at(ref, bundle, owner, count=1):
        s, parts, cut, cuts, y, ys = bundle
        first, size = (owner * CH + 2 * y, 2 * ys) if count == 1 else (0, 2 * ys * count)
        return ref.at[pl.ds(s, parts), pl.ds(cut, cuts), pl.ds(first, size), :]

    def pcol_own(e, bundle, src, dst):
        sem = pcol_sems.at[2, numbers[e, bundle]]
        return pltpu.make_async_copy(pcol_at(src, bundle, me_p), pcol_at(dst, bundle, me_p), sem)

    def pcol_start(e, bundle, src, dst):
        number = numbers.setdefault((e, bundle), len(numbers))

        def send(k, _):
            to = lax.rem(me_p + k, PC)
            band = lax.rem(work + lax.rem(to // 2, 2), 2) if e == 0 else work
            pltpu.make_async_remote_copy(
                src_ref=pcol_at(src, bundle, to),
                dst_ref=pcol_at(dst, bundle, me_p),
                send_sem=pcol_sems.at[0, number],
                recv_sem=pcol_sems.at[1, number],
                device_id={"pcol": to, "band": band},
                device_id_type=MESH,
            ).start()
            return 0

        own = pcol_own(e, bundle, src, dst)
        if e == 0:
            for k in range(1, PC):
                send(k, 0)
            own.start()
        else:
            lax.fori_loop(1 - half, PC, send, 0)
            pl.when(half == 0)(own.start)

    def pcol_all(which, e, bundle, ref):
        def wait_for(count):
            part = pcol_at(ref, bundle, 0, count)
            return pltpu.make_async_copy(part, part, pcol_sems.at[which, numbers[e, bundle]]).wait

        if e == 0:
            wait_for(PC - 1)()
        else:
            pl.when(half == 0)(wait_for(PC - 1))
            pl.when(half == 1)(wait_for(PC))

    waited = set()

    def pcol_wait(e, bundle, src, dst):
        if (e, bundle) in waited:
            return
        waited.add((e, bundle))
        own = pcol_own(e, bundle, src, dst)
        if e == 0:
            own.wait()
        else:
            pl.when(half == 0)(own.wait)
        pcol_all(1, e, bundle, dst)

    def pcol_sent(e, bundle, src):
        pcol_all(0, e, bundle, src)

    Y_PIECES = (3, 3, 3)

    def forward_bundles(s, cut):
        if cut < len(Y_PIECES):
            return [(0, PARTS, cut, 1, y, YB // Y_PIECES[cut]) for y in range(0, YB, YB // Y_PIECES[cut])]
        return [(s, 1, cut, 1, 0, YB)]

    def back_bundles(s, cut):
        if s == PARTS - 1:
            return [(s, 1, cut, 1, y, 4) for y in range(0, YB, 4)]
        return [(s, 1, cut, 1, 0, YB)]

    def prow_start(e, s, cut, src, dst):
        def send(k, _):
            to = lax.rem(me_r + k, PR)
            pltpu.make_async_remote_copy(
                src_ref=src.at[s, to, cut],
                dst_ref=dst.at[s, me_r, cut],
                send_sem=send_sem.at[e, s, cut],
                recv_sem=recv_sem.at[e, s, cut],
                device_id={"prow": to},
                device_id_type=MESH,
            ).start()
            return 0

        for k in range(1, PR):
            send(k, 0)
        pltpu.make_async_copy(src.at[s, me_r, cut], dst.at[s, me_r, cut], own_sem.at[e, s, cut]).start()

    def prow_wait(e, s, cut, src, dst):
        pltpu.make_async_copy(src.at[s, me_r, cut], dst.at[s, me_r, cut], own_sem.at[e, s, cut]).wait()
        others = dst.at[s, pl.ds(0, PR - 1), cut]
        pltpu.make_async_copy(others, others, recv_sem.at[e, s, cut]).wait()

    def prow_sent(e, s, cut, src):
        others = src.at[s, pl.ds(0, PR - 1), cut]
        pltpu.make_async_copy(others, others, send_sem.at[e, s, cut]).wait()

    def forward_z(cut):
        def step(group, _):
            dens = []
            for y4 in range(4):
                y = group * 4 + y4
                dens += pair_density(pl.ds(pl.multiple_of(cut * rows + y * XC, 16), XC))
            spec = dot3(table(0), halves(jnp.concatenate(dens, axis=0)), NT)
            spec = swap_slots([spec[k * 96 : (k + 1) * 96] for k in range(K4)], 32)
            for y4 in range(4):
                for c in range(2):
                    for s in range(PARTS):
                        first = (c * PARTS + s) * PC
                        s1[s, cut, pl.ds((group * 4 + y4) * 2 + c, PC, stride=CH), :] = spec[y4][first : first + PC]
            return 0

        for piece in range(BAND_PIECES[cut]):
            band_copy(cut, piece).wait_recv()
            groups = YB // 4 // BAND_PIECES[cut]
            lax.fori_loop(piece * groups, (piece + 1) * groups, step, 0)
            for s in range(PARTS):
                for bundle in forward_bundles(s, cut):
                    ready = (piece + 1) * groups * 4
                    if bundle[4] + bundle[5] <= ready and (0, bundle) not in numbers:
                        pcol_start(0, bundle, s1, r1)

    def forward_y(parts, cut):
        for s in parts:
            for bundle in forward_bundles(s, cut):
                pcol_wait(0, bundle, s1, r1)
        turned = jnp.concatenate([r1[s, cut].T for s in parts], axis=0)
        spec = dot3(halves(turned), table(1), NN)
        for i, s in enumerate(parts):
            blocks = swap_slots([spec[i * 128 + m * XC : i * 128 + (m + 1) * XC] for m in range(8)], XB)
            for w in range(8):
                s2[s, w // 2, cut, (w % 2) * XC : (w % 2 + 1) * XC, :] = blocks[w]
            prow_start(1, s, cut, s2, r2)

    def middle_x(s):
        for cut in range(CUTS):
            prow_wait(1, s, cut, s2, r2)
        data = r2[s].reshape(W, W)
        freq = dot3(table(2), halves(data), NN)
        freq = jnp.concatenate([freq[:N] * weight[s], freq[N:] * weight[s]], axis=0)
        back = dot3(table(3), halves(freq), NN)
        s3[s] = back.reshape(PR, CUTS, 2 * XC, W)
        for cut in range(CUTS):
            prow_start(2, s, cut, s3, r3)

    def backward_y(s, cuts):
        data = []
        for cut in cuts:
            prow_wait(2, s, cut, s3, r3)
            data += swap_slots([r3[s, w // 2, cut, (w % 2) * XC : (w % 2 + 1) * XC, :] for w in range(8)], XB)
        back = dot3(table(4), halves(jnp.concatenate(data, axis=0)), NT)
        for i, cut in enumerate(cuts):
            s4[s, cut] = back[:, i * 128 : (i + 1) * 128]
            for bundle in back_bundles(s, cut):
                pcol_start(3, bundle, s4, r4)

    def backward_z(cut):
        def step(group, _):
            near = [
                jnp.concatenate(
                    [
                        r4[s, cut, pl.ds((group * 4 + y4) * 2 + c, PC, stride=CH), :]
                        for c in range(2)
                        for s in range(PARTS)
                    ],
                    axis=0,
                )
                for y4 in range(4)
            ]
            near = jnp.concatenate(swap_slots(near, 32), axis=0)
            field = dot3(halves(near.T), table(5), NN)
            for y4 in range(4):
                y = group * 4 + y4
                source = psi[pl.ds(pl.multiple_of(cut * rows + y * XC, 16), XC), :]
                at = pl.ds(pl.multiple_of(y * XB + cut * XC, 16), XC)
                for j in range(2):
                    first = (y4 * 2 + j) * XC
                    term = field[first : first + XC] * source
                    rest = term[:, 256:]
                    out_ref[j, at, :128] = term[:, :128] + term[:, 128:256]
                    out_ref[j, at, 128:] = (rest + pltpu.roll(rest, 64, 1))[:, :64]
            return 0

        for group in range(YB // 4):
            for s in range(PARTS):
                bundles = back_bundles(s, cut)
                pcol_wait(3, bundles[group % len(bundles)], s4, r4)
            step(group, 0)

    for load in loads[CUTS:]:
        load.wait()
    for s in range(PARTS):
        block = jnp.concatenate([ker[s * K4 + m // 2] for m in range(8)], axis=0)
        weight[s] = jnp.concatenate([block, jnp.zeros((W, 64), F32)], axis=1).T[:N]
    forward_z(0)
    forward_z(1)
    forward_y((0, 1, 2), 0)
    forward_z(2)
    forward_y((0, 1, 2), 1)
    forward_y((0,), 2)
    forward_y((1,), 2)
    forward_y((2,), 2)
    middle_x(0)
    middle_x(1)
    middle_x(2)
    for part in (0, 1):
        for cut in range(CUTS):
            backward_y(part, (cut,))
    for cut in range(CUTS):
        backward_y(2, (cut,))
    for cut in range(CUTS):
        backward_z(cut)

    for cut in range(CUTS):
        for piece in range(BAND_PIECES[cut]):
            band_copy(cut, piece).wait_send()
        for s in range(PARTS):
            prow_sent(1, s, cut, s2)
            prow_sent(2, s, cut, s3)
    for e, bundle in numbers:
        pcol_sent(e, bundle, s1 if e == 0 else s4)


def on_device(orbitals, kernel, plan, occupation):
    orb = jnp.transpose(orbitals, (0, 2, 1, 3))
    ker = jnp.transpose(kernel, (1, 0, 2))
    tables = jnp.asarray(np.stack(make_tables()))
    pcol_buf = pltpu.VMEM((PARTS, CUTS, PC * CH, 128), F32)
    prow_buf = pltpu.VMEM((PARTS, PR, CUTS, 2 * XC, W), F32)
    vmem = pl.BlockSpec(memory_space=pltpu.VMEM)
    out = pl.pallas_call(
        body,
        out_shape=jax.ShapeDtypeStruct((2, YB * XB, N), F32),
        in_specs=[pl.BlockSpec(memory_space=pltpu.SMEM)] * 2 + [pl.BlockSpec(memory_space=pl.ANY)] * 3,
        out_specs=vmem,
        scratch_shapes=[
            pltpu.VMEM((CUTS, 2, YB, XC, N), F32),
            pltpu.VMEM((YB, XB, N), F32),
            pltpu.VMEM((PARTS, N, W), F32),
            pltpu.VMEM((12, W, W), BF16),
            pltpu.VMEM((YB * XB, W), F32),
            pltpu.VMEM((YB * XB, W), F32),
            pltpu.VMEM((YB * XB, W), F32),
            pcol_buf, pcol_buf, prow_buf, prow_buf, prow_buf, prow_buf, pcol_buf, pcol_buf,
            pltpu.SemaphoreType.DMA((10,)),
            pltpu.SemaphoreType.DMA((3, 32)),
            pltpu.SemaphoreType.DMA((CUTS, 3)),
            pltpu.SemaphoreType.DMA((CUTS, 3)),
            pltpu.SemaphoreType.DMA((4, PARTS, CUTS)),
            pltpu.SemaphoreType.DMA((4, PARTS, CUTS)),
            pltpu.SemaphoreType.DMA((4, PARTS, CUTS)),
        ],
        compiler_params=pltpu.CompilerParams(
            collective_id=0, has_side_effects=True, vmem_limit_bytes=56 * 2**20
        ),
    )(plan, occupation, orb, ker, tables)
    return jnp.transpose(out.reshape(2, YB, XB, N), (0, 2, 1, 3))


def solution(mesh):
    return jax.shard_map(
        on_device,
        mesh=mesh,
        in_specs=(P("band", "prow", "pcol", None), P("prow", "pcol", None), P(), P()),
        out_specs=P("band", "prow", "pcol", None),
        check_vma=False,
    )
```

```python
import functools

import jax
import jax.numpy as jnp
import ml_dtypes
import numpy as np
from jax import lax
from jax.experimental import pallas as pl
from jax.experimental.pallas import tpu as pltpu
from jax.sharding import PartitionSpec as P

N = 192
PC = 16
PR = 4
YB = 12
XB = 48
PARTS = 3
K4 = 4
CUTS = 3
XC = 16
BAND_PIECES = (3, 3, 3)
W = 384
CH = 24
F32 = jnp.float32
BF16 = jnp.bfloat16
MESH = pl.DeviceIdType.MESH


def split_table(table):
    high = table.astype(np.float32).astype(ml_dtypes.bfloat16)
    low = (table - high.astype(np.float64)).astype(np.float32).astype(ml_dtypes.bfloat16)
    return high, low


def complex_table(out_part, out_freq, in_part, in_point, sign):
    angle = 2.0 * np.pi * ((out_freq[:, None] * in_point[None, :]) % N) / N
    cosine, sine = np.cos(angle), sign * np.sin(angle)
    op, ip = out_part[:, None], in_part[None, :]
    return np.where(op == ip, cosine, np.where(op == 0, -sine, sine))


def grid(*sizes):
    return [a.reshape(-1) for a in np.meshgrid(*[np.arange(s) for s in sizes], indexing="ij")]


def make_tables():
    z_part = np.concatenate([np.zeros(128), np.ones(128), np.zeros(64), np.ones(64)]).astype(int)
    z_point = np.concatenate([np.arange(128)] * 2 + [np.arange(128, 192)] * 2)
    k4, c, s, q = grid(K4, 2, PARTS, PC)
    kz = q * YB + s * K4 + k4
    t1 = complex_table(c, kz, z_part, z_point, -1)
    t5 = -0.25 * complex_table(z_part, z_point, c, kz, 1).T
    p, y, yc = grid(PC, YB, 2)
    y_point = p * YB + y
    u, uc, k = grid(PR, 2, XB)
    ky = u * XB + k
    t2 = complex_table(uc, ky, yc, y_point, -1).T
    t4 = complex_table(yc, y_point, uc, ky, 1)
    xc, kx = grid(2, N)
    v, cut, vc, x = grid(PR, CUTS, 2, XC)
    x_point = v * XB + cut * XC + x
    t3 = complex_table(xc, kx, vc, x_point, -1)
    t3i = complex_table(vc, x_point, xc, kx, 1) / float(N) ** 3
    return [part for t in (t1, t2, t3, t3i, t4, t5) for part in split_table(t)]


def halves(x):
    high = x.astype(BF16)
    return high, (x - high.astype(F32)).astype(BF16)


def dot3(left, right, dims):
    (left_dim,), (right_dim,) = dims
    long_left = jnp.concatenate([left[0], left[0], left[1]], axis=left_dim)
    long_right = jnp.concatenate([right[0], right[1], right[0]], axis=right_dim)
    return lax.dot_general(long_left, long_right, (dims, ((), ())), preferred_element_type=F32)


NN = ((1,), (0,))
NT = ((1,), (1,))


def swap_slots(blocks, width):
    count = len(blocks)
    lanes = count * width
    slot = lax.broadcasted_iota(jnp.int32, blocks[0].shape, 1) // width
    blocks = list(blocks)
    bit = 1
    while bit < count:
        keep = (slot & bit) == 0
        for m in range(count):
            if m & bit == 0:
                a, b = blocks[m], blocks[m + bit]
                blocks[m] = jnp.where(keep, a, pltpu.roll(b, width * bit, 1))
                blocks[m + bit] = jnp.where(keep, pltpu.roll(a, lanes - width * bit, 1), b)
        bit *= 2
    return blocks


def body(
    plan_ref, occ_ref, orb_hbm, ker_hbm, tables_hbm,
    out_ref,
    orb, result, ker, weight, tables, mine, other, psi, s1, r1, s2, r2, s3, r3, s4, r4,
    load_sem, put_sem, pcol_sems, psi_send, psi_recv, own_sem, send_sem, recv_sem,
):
    def table(t):
        return tables[2 * t], tables[2 * t + 1]

    me_p = lax.axis_index("pcol")
    me_r = lax.axis_index("prow")
    me_b = lax.axis_index("band")
    half = lax.rem(me_p // 2, 2)
    work = lax.rem(me_b + half, 2)
    partner = 1 - me_b

    barrier = pltpu.get_barrier_semaphore()

    def greet_p(k, _):
        to = lax.rem(me_p + k, PC)
        band = lax.rem(work + lax.rem(to // 2, 2), 2)
        pl.semaphore_signal(barrier, inc=1, device_id={"pcol": to, "band": band}, device_id_type=MESH)
        return 0

    def greet_r(k, _):
        pl.semaphore_signal(barrier, inc=1, device_id={"prow": lax.rem(me_r + k, PR)}, device_id_type=MESH)
        return 0

    loads = [
        pltpu.make_async_copy(orb_hbm.at[:, :, pl.ds(cut * XC, XC), :], orb.at[cut], load_sem.at[cut])
        for cut in range(CUTS)
    ]
    loads += [
        pltpu.make_async_copy(
            tables_hbm.at[pl.ds(2 * t, 2)], tables.at[pl.ds(2 * t, 2)], load_sem.at[4 + t]
        )
        for t in range(6)
    ]
    loads.append(pltpu.make_async_copy(ker_hbm, ker, load_sem.at[3]))
    for load in loads[: CUTS + 1]:
        load.start()
    pl.semaphore_signal(barrier, inc=1, device_id={"band": partner}, device_id_type=MESH)
    for k in range(1, PC):
        greet_p(k, 0)
    for k in range(1, PR):
        greet_r(k, 0)

    rows = YB * XC

    def band_copy(cut, piece):
        size = rows // BAND_PIECES[cut]
        at = pl.ds(cut * rows + piece * size, size)
        return pltpu.make_async_remote_copy(
            src_ref=mine.at[at],
            dst_ref=other.at[at],
            send_sem=psi_send.at[cut, piece],
            recv_sem=psi_recv.at[cut, piece],
            device_id={"band": partner},
            device_id_type=MESH,
        )

    for cut in range(CUTS):
        loads[cut].wait()
        for y in range(YB):
            at = pl.ds(cut * rows + y * XC, XC)
            mine[at, :128] = orb[cut, 0, y, :, :128]
            mine[at, 128:256] = orb[cut, 1, y, :, :128]
            mine[at, 256:] = jnp.concatenate([orb[cut, 0, y, :, 128:], orb[cut, 1, y, :, 128:]], axis=1)
            if cut == 0 and y == YB // BAND_PIECES[0] - 1:
                pl.semaphore_wait(barrier, 1 + PC - 1 + PR - 1)
            if (y + 1) % (YB // BAND_PIECES[cut]) == 0:
                band_copy(cut, (y + 1) // (YB // BAND_PIECES[cut]) - 1).start()
    for load in loads[CUTS + 1 :]:
        load.start()

    share = [
        [
            [
                jnp.where(
                    jnp.logical_and(plan_ref[r] == 2 * owner + t, occ_ref[2 * owner + t] != 0),
                    jnp.float32(1.0), jnp.float32(0.0),
                )
                for t in range(2)
            ]
            for owner in (me_b, partner)
        ]
        for r in range(2)
    ]
    first_half = lax.broadcasted_iota(jnp.int32, (XC, 128), 1) < 64
    straight = [jnp.where(first_half, share[0][g][0], share[1][g][1]) for g in range(2)]
    crossed = [jnp.where(first_half, share[0][g][1], share[1][g][0]) for g in range(2)]

    def pair_density(at):
        tiles = []
        for ref in (mine, other):
            high = ref[at, 256:]
            tiles.append((ref[at, :128], ref[at, 128:256], high, pltpu.roll(high, 64, 1)))
        source = [
            sum(share[r][g][t] * tiles[g][t] for g in range(2) for t in range(2)) for r in range(2)
        ]
        source.append(sum(straight[g] * tiles[g][2] + crossed[g] * tiles[g][3] for g in range(2)))
        for n in range(3):
            psi[at, n * 128 : (n + 1) * 128] = source[n]
        low0, low1, high, turned = [jnp.where(half == 1, b, a) for a, b in zip(*tiles)]
        phi = [(low0, jnp.where(first_half, high, turned)), (low1, jnp.where(first_half, turned, high))]
        return [
            jnp.concatenate([low * source[0], low * source[1], up * source[2]], axis=1) for low, up in phi
        ]

    numbers = {}

    def pcol_at(ref, bundle, owner, count=1):
        s, parts, cut, cuts, y, ys = bundle
        first, size = (owner * CH + 2 * y, 2 * ys) if count == 1 else (0, 2 * ys * count)
        return ref.at[pl.ds(s, parts), pl.ds(cut, cuts), pl.ds(first, size), :]

    def pcol_own(e, bundle, src, dst):
        sem = pcol_sems.at[2, numbers[e, bundle]]
        return pltpu.make_async_copy(pcol_at(src, bundle, me_p), pcol_at(dst, bundle, me_p), sem)

    def pcol_start(e, bundle, src, dst):
        number = numbers.setdefault((e, bundle), len(numbers))

        def send(k, _):
            to = lax.rem(me_p + k, PC)
            band = lax.rem(work + lax.rem(to // 2, 2), 2) if e == 0 else work
            pltpu.make_async_remote_copy(
                src_ref=pcol_at(src, bundle, to),
                dst_ref=pcol_at(dst, bundle, me_p),
                send_sem=pcol_sems.at[0, number],
                recv_sem=pcol_sems.at[1, number],
                device_id={"pcol": to, "band": band},
                device_id_type=MESH,
            ).start()
            return 0

        own = pcol_own(e, bundle, src, dst)
        if e == 0:
            for k in range(1, PC):
                send(k, 0)
            own.start()
        else:
            lax.fori_loop(1 - half, PC, send, 0)
            pl.when(half == 0)(own.start)

    def pcol_all(which, e, bundle, ref):
        def wait_for(count):
            part = pcol_at(ref, bundle, 0, count)
            return pltpu.make_async_copy(part, part, pcol_sems.at[which, numbers[e, bundle]]).wait

        if e == 0:
            wait_for(PC - 1)()
        else:
            pl.when(half == 0)(wait_for(PC - 1))
            pl.when(half == 1)(wait_for(PC))

    waited = set()

    def pcol_wait(e, bundle, src, dst):
        if (e, bundle) in waited:
            return
        waited.add((e, bundle))
        own = pcol_own(e, bundle, src, dst)
        if e == 0:
            own.wait()
        else:
            pl.when(half == 0)(own.wait)
        pcol_all(1, e, bundle, dst)

    def pcol_sent(e, bundle, src):
        pcol_all(0, e, bundle, src)

    Y_PIECES = (3, 3, 3)

    def forward_bundles(s, cut):
        if cut < len(Y_PIECES):
            return [(0, PARTS, cut, 1, y, YB // Y_PIECES[cut]) for y in range(0, YB, YB // Y_PIECES[cut])]
        return [(s, 1, cut, 1, 0, YB)]

    def back_bundle(s, cut):
        return (s, 1, 0, CUTS, 0, YB) if s < 0 else (s, 1, cut, 1, 0, YB)

    def prow_start(e, s, cut, src, dst):
        def send(k, _):
            to = lax.rem(me_r + k, PR)
            pltpu.make_async_remote_copy(
                src_ref=src.at[s, to, cut],
                dst_ref=dst.at[s, me_r, cut],
                send_sem=send_sem.at[e, s, cut],
                recv_sem=recv_sem.at[e, s, cut],
                device_id={"prow": to},
                device_id_type=MESH,
            ).start()
            return 0

        for k in range(1, PR):
            send(k, 0)
        pltpu.make_async_copy(src.at[s, me_r, cut], dst.at[s, me_r, cut], own_sem.at[e, s, cut]).start()

    def prow_wait(e, s, cut, src, dst):
        pltpu.make_async_copy(src.at[s, me_r, cut], dst.at[s, me_r, cut], own_sem.at[e, s, cut]).wait()
        others = dst.at[s, pl.ds(0, PR - 1), cut]
        pltpu.make_async_copy(others, others, recv_sem.at[e, s, cut]).wait()

    def prow_sent(e, s, cut, src):
        others = src.at[s, pl.ds(0, PR - 1), cut]
        pltpu.make_async_copy(others, others, send_sem.at[e, s, cut]).wait()

    def forward_z(cut):
        def step(group, _):
            dens = []
            for y4 in range(4):
                y = group * 4 + y4
                dens += pair_density(pl.ds(pl.multiple_of(cut * rows + y * XC, 16), XC))
            spec = dot3(table(0), halves(jnp.concatenate(dens, axis=0)), NT)
            spec = swap_slots([spec[k * 96 : (k + 1) * 96] for k in range(K4)], 32)
            for y4 in range(4):
                for c in range(2):
                    for s in range(PARTS):
                        first = (c * PARTS + s) * PC
                        s1[s, cut, pl.ds((group * 4 + y4) * 2 + c, PC, stride=CH), :] = spec[y4][first : first + PC]
            return 0

        for piece in range(BAND_PIECES[cut]):
            band_copy(cut, piece).wait_recv()
            groups = YB // 4 // BAND_PIECES[cut]
            lax.fori_loop(piece * groups, (piece + 1) * groups, step, 0)
            for s in range(PARTS):
                for bundle in forward_bundles(s, cut):
                    ready = (piece + 1) * groups * 4
                    if bundle[4] + bundle[5] <= ready and (0, bundle) not in numbers:
                        pcol_start(0, bundle, s1, r1)

    def forward_y(parts, cut):
        for s in parts:
            for bundle in forward_bundles(s, cut):
                pcol_wait(0, bundle, s1, r1)
        turned = jnp.concatenate([r1[s, cut].T for s in parts], axis=0)
        spec = dot3(halves(turned), table(1), NN)
        for i, s in enumerate(parts):
            blocks = swap_slots([spec[i * 128 + m * XC : i * 128 + (m + 1) * XC] for m in range(8)], XB)
            for w in range(8):
                s2[s, w // 2, cut, (w % 2) * XC : (w % 2 + 1) * XC, :] = blocks[w]
            prow_start(1, s, cut, s2, r2)

    def middle_x(s):
        for cut in range(CUTS):
            prow_wait(1, s, cut, s2, r2)
        data = r2[s].reshape(W, W)
        freq = dot3(table(2), halves(data), NN)
        freq = jnp.concatenate([freq[:N] * weight[s], freq[N:] * weight[s]], axis=0)
        back = dot3(table(3), halves(freq), NN)
        s3[s] = back.reshape(PR, CUTS, 2 * XC, W)
        for cut in range(CUTS):
            prow_start(2, s, cut, s3, r3)

    def backward_y(s, cuts):
        data = []
        for cut in cuts:
            prow_wait(2, s, cut, s3, r3)
            data += swap_slots([r3[s, w // 2, cut, (w % 2) * XC : (w % 2 + 1) * XC, :] for w in range(8)], XB)
        back = dot3(table(4), halves(jnp.concatenate(data, axis=0)), NT)
        for i, cut in enumerate(cuts):
            s4[s, cut] = back[:, i * 128 : (i + 1) * 128]
            if cut == CUTS - 1 or back_bundle(s, cut) != back_bundle(s, cut + 1):
                pcol_start(3, back_bundle(s, cut), s4, r4)

    def put(cut):
        return pltpu.make_async_copy(result.at[cut], out_ref.at[:, :, pl.ds(cut * XC, XC), :], put_sem.at[cut])

    def backward_z(cut):
        def step(group, _):
            near = [
                jnp.concatenate(
                    [
                        r4[s, cut, pl.ds((group * 4 + y4) * 2 + c, PC, stride=CH), :]
                        for c in range(2)
                        for s in range(PARTS)
                    ],
                    axis=0,
                )
                for y4 in range(4)
            ]
            near = jnp.concatenate(swap_slots(near, 32), axis=0)
            field = dot3(halves(near.T), table(5), NN)
            for y4 in range(4):
                y = group * 4 + y4
                source = psi[pl.ds(pl.multiple_of(cut * rows + y * XC, 16), XC), :]
                for j in range(2):
                    first = (y4 * 2 + j) * XC
                    term = field[first : first + XC] * source
                    rest = term[:, 256:]
                    result[cut, j, y, :, :128] = term[:, :128] + term[:, 128:256]
                    result[cut, j, y, :, 128:] = (rest + pltpu.roll(rest, 64, 1))[:, :64]
            return 0

        for s in range(PARTS):
            pcol_wait(3, back_bundle(s, cut), s4, r4)
        lax.fori_loop(0, YB // 4, step, 0)
        put(cut).start()

    loads[CUTS].wait()
    forward_z(0)
    for load in loads[CUTS + 1 :]:
        load.wait()
    forward_z(1)
    for s in range(PARTS):
        block = jnp.concatenate([ker[s * K4 + m // 2] for m in range(8)], axis=0)
        weight[s] = jnp.concatenate([block, jnp.zeros((W, 64), F32)], axis=1).T[:N]
    forward_y((0, 1, 2), 0)
    forward_z(2)
    forward_y((0, 1, 2), 1)
    forward_y((0,), 2)
    forward_y((1,), 2)
    forward_y((2,), 2)
    middle_x(0)
    middle_x(1)
    middle_x(2)
    for part in (0, 1):
        for cut in range(CUTS):
            backward_y(part, (cut,))
    for cut in range(CUTS):
        backward_y(2, (cut,))
    for cut in range(CUTS):
        backward_z(cut)

    for cut in range(CUTS):
        put(cut).wait()
        for piece in range(BAND_PIECES[cut]):
            band_copy(cut, piece).wait_send()
        for s in range(PARTS):
            prow_sent(1, s, cut, s2)
            prow_sent(2, s, cut, s3)
    for e, bundle in numbers:
        pcol_sent(e, bundle, s1 if e == 0 else s4)


def on_device(orbitals, kernel, plan, occupation):
    orb = jnp.transpose(orbitals, (0, 2, 1, 3))
    ker = jnp.transpose(kernel, (1, 0, 2))
    tables = jnp.asarray(np.stack(make_tables()))
    pcol_buf = pltpu.VMEM((PARTS, CUTS, PC * CH, 128), F32)
    prow_buf = pltpu.VMEM((PARTS, PR, CUTS, 2 * XC, W), F32)
    out = pl.pallas_call(
        body,
        out_shape=jax.ShapeDtypeStruct((2, YB, XB, N), F32),
        in_specs=[pl.BlockSpec(memory_space=pltpu.SMEM)] * 2 + [pl.BlockSpec(memory_space=pl.ANY)] * 3,
        out_specs=pl.BlockSpec(memory_space=pl.ANY),
        scratch_shapes=[
            pltpu.VMEM((CUTS, 2, YB, XC, N), F32),
            pltpu.VMEM((CUTS, 2, YB, XC, N), F32),
            pltpu.VMEM((YB, XB, N), F32),
            pltpu.VMEM((PARTS, N, W), F32),
            pltpu.VMEM((12, W, W), BF16),
            pltpu.VMEM((YB * XB, W), F32),
            pltpu.VMEM((YB * XB, W), F32),
            pltpu.VMEM((YB * XB, W), F32),
            pcol_buf, pcol_buf, prow_buf, prow_buf, prow_buf, prow_buf, pcol_buf, pcol_buf,
            pltpu.SemaphoreType.DMA((10,)),
            pltpu.SemaphoreType.DMA((CUTS,)),
            pltpu.SemaphoreType.DMA((3, 24)),
            pltpu.SemaphoreType.DMA((CUTS, 3)),
            pltpu.SemaphoreType.DMA((CUTS, 3)),
            pltpu.SemaphoreType.DMA((4, PARTS, CUTS)),
            pltpu.SemaphoreType.DMA((4, PARTS, CUTS)),
            pltpu.SemaphoreType.DMA((4, PARTS, CUTS)),
        ],
        compiler_params=pltpu.CompilerParams(
            collective_id=0, has_side_effects=True, vmem_limit_bytes=56 * 2**20
        ),
    )(plan, occupation, orb, ker, tables)
    return jnp.transpose(out, (0, 2, 1, 3))


def solution(mesh):
    return jax.shard_map(
        on_device,
        mesh=mesh,
        in_specs=(P("band", "prow", "pcol", None), P("prow", "pcol", None), P(), P()),
        out_specs=P("band", "prow", "pcol", None),
        check_vma=False,
    )
```
